32 devices in a mesh: blk: 16 (over z, x, core), tgt: 2 (over y).
Axes of the slice: x: 2, y: 2, z: 4, core: 2. Of those that a mesh axis runs over, the one named last changes fastest.
Arguments:
- gradients: bfloat16 [8192, 8192], P('blk', 'tgt'), may hold values from -6 to 6
- targets: bfloat16 [8192, 64], P('blk'), may hold values from -0.15625 to 0.15625
Outputs:
- kernel_tiles: bfloat16 [3, 8192, 512], P(None, ('blk', 'tgt'))
- influence: float32 [8192, 64], P(('blk', 'tgt'))
The draws below stay inside these ranges and needn't reach their ends.
All inputs are finite; a program needn't handle non-finite values.
Results may differ from the reference program's by a relative error of at most 0.0029.
Values may be sent and summed in bfloat16 or wider, within the bound.
No kernel may reach another device: no remote copies, remote signals or barrier semaphores. Data moves between devices by JAX's collectives and lax.ppermute only.
A program may use at most 64 MiB of HBM per device.

```python
import jax
import jax.numpy as jnp
from jax import lax

P_SIZE = 8192
C = 64
E = 512
ROUNDS = 2
EXAMPLES = 8192
N_BLK = 16


def levels(rng, dims, cuts, least, high):
    factor_of = 1.0
    for axis_at, parts in cuts:
        heights = jax.random.uniform(jax.random.fold_in(jax.random.fold_in(rng, 6), axis_at), (parts,), jnp.float32, least / len(cuts), high / len(cuts))
        factor_of = factor_of * jnp.repeat(jnp.exp(heights), dims[axis_at] // parts).reshape((-1,) + (1,) * (len(dims) - 1 - axis_at))
    return factor_of


def gaussian(key, shape, deviation, reach, split=(), held_as=jnp.bfloat16):
    level = levels(key, shape, split, -0.22, 0.18) if split else 1.0
    array = jax.random.normal(key, shape, jnp.float32) * deviation * level
    return jnp.minimum(jnp.maximum(array, -reach), reach).astype(held_as)


def setup_inputs(seed: int = 0) -> dict:
    keys = jax.random.split(jax.random.key(seed), 3)
    gradients = gaussian(keys[0], (EXAMPLES, P_SIZE), 1.0, 6.0, ((0, 16), (1, 2)))
    targets = gaussian(keys[1], (EXAMPLES, C), (E * (ROUNDS + 1)) ** -0.5, 0.15625, ((0, 16),))
    return dict(gradients=gradients, targets=targets)


def reference(gradients, targets):
    scale = 1.0 / (P_SIZE ** 0.5)
    grads_blocks = gradients.reshape(N_BLK, E, P_SIZE)
    targ_blocks = targets.reshape(N_BLK, E, C)

    def self_work(index):
        own = grads_blocks[index]
        kernel = (jnp.dot(own, own.T, preferred_element_type=jnp.float32) * scale).astype(jnp.bfloat16)
        return kernel, jnp.dot(kernel, targ_blocks[index], preferred_element_type=jnp.float32)

    self_tiles, self_out = lax.map(self_work, jnp.arange(N_BLK, dtype=jnp.int32))
    tile_list = [self_tiles.reshape(N_BLK * E, E)]
    influence = self_out.reshape(N_BLK * E, C)
    for level in range(ROUNDS):
        stride = 2 ** level
        groups = N_BLK // (2 * stride)
        grads_five = gradients.reshape(groups, 2, stride, E, P_SIZE)
        targ_five = targets.reshape(groups, 2, stride, E, C)

        def pair_work(index):
            group = index // stride
            member = index % stride
            lower = grads_five[group, 0, member]
            upper = grads_five[group, 1, member]
            kernel = (jnp.dot(lower, upper.T, preferred_element_type=jnp.float32) * scale).astype(jnp.bfloat16)
            low_out = jnp.dot(kernel, targ_five[group, 1, member], preferred_element_type=jnp.float32)
            high_out = jnp.dot(kernel.T, targ_five[group, 0, member], preferred_element_type=jnp.float32)
            return kernel, kernel.T, low_out, high_out

        low_tile, high_tile, low_out, high_out = lax.map(pair_work, jnp.arange(N_BLK // 2, dtype=jnp.int32))
        tiles = jnp.stack([low_tile.reshape(groups, stride, E, E), high_tile.reshape(groups, stride, E, E)], 1)
        tile_list.append(tiles.reshape(N_BLK * E, E))
        outs = jnp.stack([low_out.reshape(groups, stride, E, C), high_out.reshape(groups, stride, E, C)], 1)
        influence = influence + outs.reshape(N_BLK * E, C)
    return jnp.stack(tile_list, 0), influence
```

```python
import jax
import jax.numpy as jnp
from jax import lax
from jax.sharding import PartitionSpec as P

AFTER = {0: 1, 1: 3, 3: 2, 2: 0}
BEFORE = {after: before for before, after in AFTER.items()}
PARTS = (64, 64, 64, 32, 32)


def contract(left, right):
    return lax.dot_general(
        left, right, (((1,), (1,)), ((), ())), preferred_element_type=jnp.float32
    )


def per_device(gradients, targets):
    blocks, groups = lax.axis_size("blk"), lax.axis_size("tgt")
    rows, features = gradients.shape
    half = rows // groups
    scale = 1.0 / (features * groups) ** 0.5
    forward = [(b, b - b % 4 + AFTER[b % 4]) for b in range(blocks)]
    back = [(b, b - b % 4 + BEFORE[b % 4]) for b in range(blocks)]
    across = [(t, 1 - t) for t in range(groups)]
    back_across = [(b * groups + t, c * groups + 1 - t) for b, c in back for t in range(groups)]
    me, t = lax.axis_index("blk"), lax.axis_index("tgt")
    other = 1 - t

    halves = gradients.reshape(groups, half, features)
    got, at, source = [], 0, halves
    for width in PARTS:
        piece = source[:, at : at + width].reshape(groups * width, features)
        source, piece = lax.optimization_barrier((source, piece))
        got.append(lax.ppermute(piece, "blk", forward))
        at += width
    targets_before = lax.ppermute(targets, "blk", forward)
    targets_after = lax.ppermute(targets, "blk", back)

    mine = lax.dynamic_slice_in_dim(gradients, t * half, half, 0)
    others = lax.dynamic_slice_in_dim(gradients, other * half, half, 0)

    sent = lax.ppermute(contract(others, gradients), "tgt", across)
    self_tile = ((contract(mine, gradients) + sent) * scale).astype(jnp.bfloat16)
    influence = jnp.dot(self_tile, targets, preferred_element_type=jnp.float32)

    columns, far = [], []
    for width, block in zip(PARTS, got):
        sent = lax.ppermute(contract(block, others), "tgt", across)
        part = ((contract(block, mine) + sent) * scale).astype(jnp.bfloat16)
        part = part.reshape(groups, width, half)
        columns.append(part)
        near = lax.dynamic_index_in_dim(part, t, 0, keepdims=False)
        cross = lax.dynamic_index_in_dim(part, other, 0, keepdims=False)
        near = lax.ppermute(near, "blk", back)
        cross = lax.ppermute(cross, ("blk", "tgt"), back_across)
        far.append(jnp.where(t == 0, jnp.concatenate([near, cross], 1), jnp.concatenate([cross, near], 1)))
    met = jnp.concatenate(columns, 1).reshape(rows, half).T
    back_tile = jnp.concatenate(far, 0)
    influence = influence + jnp.dot(met, targets_before, preferred_element_type=jnp.float32)
    influence = influence + jnp.dot(back_tile, targets_after, preferred_element_type=jnp.float32)

    first = (me % 4 == 1) | (me % 4 == 2)
    tiles = jnp.stack([self_tile, jnp.where(first, met, back_tile), jnp.where(first, back_tile, met)], 0)
    return tiles, influence


def solution(mesh):
    return jax.shard_map(
        per_device,
        mesh=mesh,
        in_specs=(P("blk", "tgt"), P("blk", None)),
        out_specs=(P(None, ("blk", "tgt"), None), P(("blk", "tgt"), None)),
        check_vma=False,
    )
```

```python
import functools

import jax
import jax.numpy as jnp
from jax import lax
from jax.experimental import pallas as pl
from jax.experimental.pallas import tpu as pltpu
from jax.sharding import PartitionSpec as P

AFTER = {0: 1, 1: 3, 3: 2, 2: 0}
BEFORE = {after: before for before, after in AFTER.items()}
SIXTEENTHS = (6, 5, 3, 2)

VMEM = pl.BlockSpec(memory_space=pltpu.VMEM)
ANY = pl.BlockSpec(memory_space=pl.ANY)
COST = pl.CostEstimate(flops=0, bytes_accessed=0, transcendentals=0)


def call(kernel, out, in_specs, out_specs, scratch=(), aliases=None, vmem=16):
    return pl.pallas_call(
        kernel,
        out_shape=out,
        in_specs=in_specs,
        out_specs=out_specs,
        scratch_shapes=scratch,
        input_output_aliases=aliases or {},
        cost_estimate=COST,
        compiler_params=pltpu.CompilerParams(vmem_limit_bytes=vmem * 2**20),
    )


def contract(left, right):
    return lax.dot_general(
        left, right, (((1,), (1,)), ((), ())), preferred_element_type=jnp.float32
    )


def multiply(left, right):
    return jnp.dot(left, right, preferred_element_type=jnp.float32)


def part_of(index, size):
    return pl.ds(pl.multiple_of(index * size, size), size)


def run_copies(copies, sems):
    copies = [pltpu.make_async_copy(*ends, sems.at[i]) for i, ends in enumerate(copies)]
    for copy in copies:
        copy.start()
    for copy in copies:
        copy.wait()


def first_kernel(width, half, grads, flat, out, sems):
    wide = out.shape[1]
    copies = [
        (
            grads.at[pl.ds(h * half, width), pl.ds(k * wide, wide)],
            out.at[pl.ds((2 * k + h) * width, width)],
        )
        for k in range(2)
        for h in range(2)
    ]
    long = flat.shape[1]
    for j in range(flat.shape[0] // 16):
        down, along = divmod(j, wide // long)
        copies.append(
            (
                flat.at[pl.ds(16 * j, 16)],
                out.at[pl.ds(4 * width + 16 * down, 16), pl.ds(along * long, long)],
            )
        )
    run_copies(copies, sems)


def rest_kernel(spans, half, grads, before, *refs):
    del before
    *outs, sems = refs
    run_copies(
        [
            (grads.at[pl.ds(h * half + at, width)], out.at[pl.ds(h * width, width)])
            for (at, width), out in zip(spans, outs)
            for h in range(2)
        ],
        sems,
    )


def self_kernel(half, grads, before, sent, kept):
    del before
    t = lax.axis_index("tgt")
    sent[...] = contract(grads[part_of(1 - t, half), :], grads[...])
    kept[...] = contract(grads[part_of(t, half), :], grads[...])


def self_finish_kernel(scale, kept, got, tile):
    tile[...] = ((kept[...] + got[...]) * scale).astype(jnp.bfloat16)


def share(sent, kept, width):
    t = lax.axis_index("tgt")
    sent[2 * width :, :] = kept[part_of(1 - t, width), :]
    kept[2 * width :, :] = sent[part_of(t, width), :]


def first_pair_kernel(width, half, columns, piece, grads, sent, kept, flat):
    wide = piece.shape[1]
    t = lax.axis_index("tgt")
    for to, index in ((sent, 1 - t), (kept, t)):
        rows = part_of(index, half)
        to[: 2 * width, :] = contract(piece[: 2 * width, :], grads[rows, :wide]) + contract(
            piece[2 * width : 4 * width, :], grads[rows, wide:]
        )
    share(sent, kept, width)
    long = flat.shape[1]
    for j in range(columns // 16):
        down, along = divmod(j, wide // long)
        flat[16 * j : 16 * j + 16, :] = piece[
            4 * width + 16 * down : 4 * width + 16 * down + 16, along * long : (along + 1) * long
        ]


def pair_kernel(width, half, piece, grads, before, sent, kept):
    del before
    t = lax.axis_index("tgt")
    sent[: 2 * width, :] = contract(piece[...], grads[part_of(1 - t, half), :])
    kept[: 2 * width, :] = contract(piece[...], grads[part_of(t, half), :])
    share(sent, kept, width)


def last_pair_kernel(width, half, piece, grads, sent, kept, near, cross):
    t = lax.axis_index("tgt")
    sent[...] = contract(piece[...], grads[part_of(1 - t, half), :])
    kept[...] = contract(piece[...], grads[part_of(t, half), :])
    for to, index in ((near, t), (cross, 1 - t)):
        to[:, part_of(t, half)] = kept[part_of(index, width), :]
        to[:, part_of(1 - t, half)] = sent[part_of(index, width), :]


def finish_kernel(widths, half, scale, *refs):
    ins, (flat, before, met, back) = refs[: 2 * len(widths)], refs[2 * len(widths) :]
    del before
    t = lax.axis_index("tgt")
    at = 0
    for i, width in enumerate(widths):
        kept, got = ins[2 * i : 2 * i + 2]
        value = ((kept[...] + got[...]) * scale).astype(jnp.bfloat16)
        for h in range(2):
            met[h * half + at : h * half + at + width, :] = value[h * width : (h + 1) * width]
        back[at : at + width, part_of(1 - t, half)] = value[2 * width :]
        at += width
    back[:at, part_of(t, half)] = met[pl.ds(pl.multiple_of(t * half, half), at), :]
    back[at:, :] = flat[...]
    for h in range(2):
        met[h * half + at : (h + 1) * half, :] = jnp.zeros((half - at, half), jnp.bfloat16)


def own_slot():
    place = lax.rem(lax.axis_index("blk"), 4)
    return jnp.where((place == 1) | (place == 2), 1, 2)


def most_kernel(half, edge, self_tile, met, flat, flat_before, tiles, partial, turned, sems):
    slot = own_slot()
    whole = pltpu.make_async_copy(self_tile, tiles.at[0], sems.at[0])
    whole.start()
    value = contract(flat[...], self_tile[...])
    copies = []
    for h in range(2):
        rows = slice(h * half, h * half + edge)
        turned[h] = met[rows, :].T
        copies.append(
            pltpu.make_async_copy(
                turned.at[h], tiles.at[slot, :, pl.ds(h * half, edge)], sems.at[1 + h]
            )
        )
        copies[h].start()
        value += multiply(flat_before[:, rows], met[rows, :])
    partial[...] = value
    whole.wait()
    for copy in copies:
        copy.wait()


def last_kernel(
    half, edge, scale, before, partial, met, back, flat_before, kept, got, near, cross,
    tiles, influence, turned, far, late, total, sems,
):
    del before
    slot = own_slot()
    rows, width = far.shape[0], near.shape[0]
    done = rows - width
    copies = [
        pltpu.make_async_copy(
            back.at[pl.ds(0, done)], tiles.at[3 - slot, pl.ds(0, done)], sems.at[0]
        )
    ]
    copies[0].start()
    far[done:, :] = ((near[...] + cross[...]) * scale).astype(jnp.bfloat16)
    copies.append(
        pltpu.make_async_copy(
            far.at[pl.ds(done, width)], tiles.at[3 - slot, pl.ds(done, width)], sems.at[1]
        )
    )
    copies[1].start()
    new = ((kept[...] + got[...]) * scale).astype(jnp.bfloat16)
    value = partial[...]
    for h in range(2):
        stop = (h + 1) * half
        late[h, : done - edge, :] = met[h * half + edge : h * half + done, :]
        late[h, done - edge :, :] = new[h * width : (h + 1) * width]
        turned[h] = late[h].T
        copies.append(
            pltpu.make_async_copy(
                turned.at[h], tiles.at[slot, :, pl.ds(h * half + edge, half - edge)], sems.at[2 + h]
            )
        )
        copies[-1].start()
        value += multiply(flat_before[:, h * half + edge : stop], late[h])
    far[:done, :] = back[:done, :]
    total[...] = value + contract(back[done:, :], far[...])
    copies.append(pltpu.make_async_copy(total, influence, sems.at[4]))
    copies[-1].start()
    for copy in copies:
        copy.wait()


def per_device(gradients, targets):
    blocks, groups = lax.axis_size("blk"), lax.axis_size("tgt")
    rows, features = gradients.shape
    columns = targets.shape[1]
    half = rows // groups
    scale = 1.0 / (features * groups) ** 0.5
    forward = [(b, b - b % 4 + AFTER[b % 4]) for b in range(blocks)]
    back = [(b, b - b % 4 + BEFORE[b % 4]) for b in range(blocks)]
    across = [(t, 1 - t) for t in range(groups)]
    back_across = [(b * groups + t, c * groups + 1 - t) for b, c in back for t in range(groups)]

    def f32(*shape):
        return jax.ShapeDtypeStruct(shape, jnp.float32)

    def b16(*shape):
        return jax.ShapeDtypeStruct(shape, jnp.bfloat16)

    widths = [half * n // 16 for n in SIXTEENTHS]
    spans = [(sum(widths[:i]), w) for i, w in enumerate(widths)]
    done = spans[-1][0]
    edge = half // 2
    flat = targets.T

    wide = features // 2
    below = 16 * -(-(columns // 16) // (wide // rows))
    piece = call(
        functools.partial(first_kernel, widths[0], half),
        b16(4 * widths[0] + below, wide),
        [ANY] * 2,
        ANY,
        [pltpu.SemaphoreType.DMA((4 + columns // 16,))],
    )(gradients, flat)
    sent, kept = call(
        functools.partial(self_kernel, half), [f32(half, rows)] * 2, [VMEM, ANY], [VMEM] * 2
    )(gradients, piece)
    pieces = call(
        functools.partial(rest_kernel, spans[1:], half),
        [b16(2 * w, features) for w in widths[1:]],
        [ANY] * 2,
        [ANY] * 3,
        [pltpu.SemaphoreType.DMA((6,))],
    )(gradients, kept)
    got = [lax.ppermute(piece, "blk", forward) for piece in (piece, *pieces)]
    self_tile = call(
        functools.partial(self_finish_kernel, scale), b16(half, rows), [VMEM] * 2, VMEM
    )(kept, lax.ppermute(sent, "tgt", across))

    sums = []
    sent, kept, flat_before = call(
        functools.partial(first_pair_kernel, widths[0], half, columns),
        [f32(3 * widths[0], half)] * 2 + [b16(columns, rows)],
        [VMEM] * 2,
        [VMEM] * 3,
    )(got[0], gradients)
    sums += [kept, lax.ppermute(sent, "tgt", across)]
    after = self_tile
    for width, piece in zip(widths[1:3], got[1:3]):
        sent, kept = call(
            functools.partial(pair_kernel, width, half),
            [f32(3 * width, half)] * 2,
            [VMEM] * 2 + [ANY],
            [VMEM] * 2,
        )(piece, gradients, after)
        sums += [kept, lax.ppermute(sent, "tgt", across)]
        after = kept
    width = widths[3]
    sent, kept, near, cross = call(
        functools.partial(last_pair_kernel, width, half),
        [f32(2 * width, half)] * 2 + [f32(width, rows)] * 2,
        [VMEM] * 2,
        [VMEM] * 4,
    )(got[3], gradients)
    last = [
        kept,
        lax.ppermute(sent, "tgt", across),
        lax.ppermute(near, "blk", back),
        lax.ppermute(cross, ("blk", "tgt"), back_across),
    ]
    met, returned = call(
        functools.partial(finish_kernel, widths[:3], half, scale),
        [b16(rows, half), b16(done + columns, rows)],
        [VMEM] * 7 + [ANY],
        [VMEM] * 2,
    )(*sums, flat, kept)
    returned = lax.ppermute(returned, "blk", back)

    tiles, partial = call(
        functools.partial(most_kernel, half, edge),
        [b16(3, half, rows), f32(columns, half)],
        [VMEM] * 4,
        [ANY, VMEM],
        [pltpu.VMEM((2, half, edge), jnp.bfloat16), pltpu.SemaphoreType.DMA((3,))],
    )(self_tile, met, flat, flat_before)
    tiles, influence = call(
        functools.partial(last_kernel, half, edge, scale),
        [b16(3, half, rows), f32(columns, half)],
        [ANY] + [VMEM] * 8,
        [ANY] * 2,
        [
            pltpu.VMEM((2, half, half - edge), jnp.bfloat16),
            pltpu.VMEM((half, rows), jnp.bfloat16),
            pltpu.VMEM((2, half - edge, half), jnp.bfloat16),
            pltpu.VMEM((columns, half), jnp.float32),
            pltpu.SemaphoreType.DMA((5,)),
        ],
        {0: 0},
    )(tiles, partial, met, returned, flat_before, *last)
    return tiles, influence.T


def solution(mesh):
    return jax.shard_map(
        per_device,
        mesh=mesh,
        in_specs=(P("blk", "tgt"), P("blk", None)),
        out_specs=(P(None, ("blk", "tgt"), None), P(("blk", "tgt"), None)),
        check_vma=False,
    )
```

```python
import functools

import jax
import jax.numpy as jnp
from jax import lax
from jax.experimental import pallas as pl
from jax.experimental.pallas import tpu as pltpu
from jax.sharding import PartitionSpec as P

AFTER = {0: 1, 1: 3, 3: 2, 2: 0}
BEFORE = {after: before for before, after in AFTER.items()}
SIXTEENTHS = (7, 5, 2, 2)

FIRST_VMEM = 50
VMEM = pl.BlockSpec(memory_space=pltpu.VMEM)
ANY = pl.BlockSpec(memory_space=pl.ANY)
COST = pl.CostEstimate(flops=0, bytes_accessed=0, transcendentals=0)


def call(kernel, out, in_specs, out_specs, scratch=(), aliases=None, vmem=16):
    return pl.pallas_call(
        kernel,
        out_shape=out,
        in_specs=in_specs,
        out_specs=out_specs,
        scratch_shapes=scratch,
        input_output_aliases=aliases or {},
        cost_estimate=COST,
        compiler_params=pltpu.CompilerParams(vmem_limit_bytes=vmem * 2**20),
    )


def contract(left, right):
    return lax.dot_general(
        left, right, (((1,), (1,)), ((), ())), preferred_element_type=jnp.float32
    )


def multiply(left, right):
    return jnp.dot(left, right, preferred_element_type=jnp.float32)


def part_of(index, size):
    return pl.ds(pl.multiple_of(index * size, size), size)


def run_copies(copies, sems):
    copies = [pltpu.make_async_copy(*ends, sems.at[i]) for i, ends in enumerate(copies)]
    for copy in copies:
        copy.start()
    for copy in copies:
        copy.wait()


def first_kernel(width, half, grads, out, mark, sems):
    run_copies(
        [
            (grads.at[pl.ds(h * half, width)], out.at[pl.ds(h * width, width)])
            for h in range(2)
        ],
        sems,
    )
    mark[...] = jnp.zeros_like(mark)


def load_kernel(grads, before, out, sems):
    del before
    size = grads.shape[0] // 4
    run_copies([(grads.at[pl.ds(i * size, size)], out.at[pl.ds(i * size, size)]) for i in range(4)], sems)


def rest_kernel(spans, half, grads, before, *refs):
    del before
    *outs, sems = refs
    run_copies(
        [
            (grads.at[pl.ds(h * half + at, width)], out.at[pl.ds(h * width, width)])
            for (at, width), out in zip(spans, outs)
            for h in range(2)
        ],
        sems,
    )


def self_kernel(half, grads, before, sent, kept):
    del before
    t = lax.axis_index("tgt")
    sent[...] = contract(grads[part_of(1 - t, half), :], grads[...])
    kept[...] = contract(grads[part_of(t, half), :], grads[...])


def self_finish_kernel(scale, kept, got, tile):
    tile[...] = ((kept[...] + got[...]) * scale).astype(jnp.bfloat16)


def share(sent, kept, width):
    t = lax.axis_index("tgt")
    sent[2 * width :, :] = kept[part_of(1 - t, width), :]
    kept[2 * width :, :] = sent[part_of(t, width), :]


def pair_kernel(width, half, piece, grads, before, sent, kept):
    del before
    t = lax.axis_index("tgt")
    sent[: 2 * width, :] = contract(piece[...], grads[part_of(1 - t, half), :])
    kept[: 2 * width, :] = contract(piece[...], grads[part_of(t, half), :])
    share(sent, kept, width)


def last_pair_kernel(width, half, scale, piece, grads, third, got, before, sent, kept, near, cross, tile):
    del before
    t = lax.axis_index("tgt")
    sent[...] = contract(piece[...], grads[part_of(1 - t, half), :])
    kept[...] = contract(piece[...], grads[part_of(t, half), :])
    for to, index in ((near, t), (cross, 1 - t)):
        to[:width, part_of(t, half)] = kept[part_of(index, width), :]
        to[:width, part_of(1 - t, half)] = sent[part_of(index, width), :]
    above = tile.shape[0] // 2
    value = (third[...] + got[...]) * scale
    tile[...] = value[: 2 * above].astype(jnp.bfloat16)
    near[width:, part_of(1 - t, half)] = value[2 * above :]
    rows = part_of(t, above)
    near[width:, part_of(t, half)] = (third[rows, :] + got[rows, :]) * scale


def finish_kernel(widths, half, scale, flat, before, *refs):
    del before
    *ins, tile, back, copy = refs
    t = lax.axis_index("tgt")
    at, total = 0, sum(widths)
    for i, width in enumerate(widths):
        kept, got = ins[2 * i : 2 * i + 2]
        value = ((kept[...] + got[...]) * scale).astype(jnp.bfloat16)
        for h in range(2):
            tile[h * total + at : h * total + at + width, :] = value[h * width : (h + 1) * width]
        back[at : at + width, part_of(1 - t, half)] = value[2 * width :]
        at += width
    back[:, part_of(t, half)] = tile[part_of(t, total), :]
    copy[...] = flat[...]


def own_slot():
    place = lax.rem(lax.axis_index("blk"), 4)
    return jnp.where((place == 1) | (place == 2), 1, 2)


def most_kernel(half, edge, self_tile, tile, flat, tiles, partial, turned, sems):
    slot = own_slot()
    whole = pltpu.make_async_copy(self_tile, tiles.at[0], sems.at[0])
    whole.start()
    partial[...] = contract(flat[...], self_tile[...])
    copies, size = [], tile.shape[0] // 2
    for h in range(2):
        part = tile[h * size : h * size + edge, :]
        turned[h] = part.T
        copies.append(
            pltpu.make_async_copy(
                turned.at[h], tiles.at[slot, :, pl.ds(h * half, edge)], sems.at[1 + h]
            )
        )
        copies[h].start()
    whole.wait()
    for copy in copies:
        copy.wait()


def last_kernel(
    half, edge, scale, before, partial, early, third, back_early, flat_before, flat_after,
    kept, got, near, cross, tiles, influence, turned, far, late, total, sems,
):
    del before
    slot = own_slot()
    width = cross.shape[0]
    first, second = early.shape[0] // 2, third.shape[0] // 2
    done = first + second
    copies = []

    def copy(source, target):
        copies.append(pltpu.make_async_copy(source, target, sems.at[len(copies)]))
        copies[-1].start()

    copy(back_early, tiles.at[3 - slot, pl.ds(0, first)])
    far[first:done, :] = near[width:, :].astype(jnp.bfloat16)
    far[done:, :] = ((near[:width, :] + cross[...]) * scale).astype(jnp.bfloat16)
    copy(
        far.at[pl.ds(first, second + width)], tiles.at[3 - slot, pl.ds(first, second + width)]
    )
    new = ((kept[...] + got[...]) * scale).astype(jnp.bfloat16)
    value = partial[...]
    for h in range(2):
        late[h, : first - edge, :] = early[h * first + edge : (h + 1) * first, :]
        late[h, first - edge : done - edge, :] = third[h * second : (h + 1) * second, :]
        late[h, done - edge :, :] = new[h * width : (h + 1) * width]
        turned[h] = late[h].T
        copy(turned.at[h], tiles.at[slot, :, pl.ds(h * half + edge, half - edge)])
        value += multiply(
            flat_before[:, h * half : h * half + edge], early[h * first : h * first + edge, :]
        ) + multiply(flat_before[:, h * half + edge : (h + 1) * half], late[h])
    far[:first, :] = back_early[...]
    total[...] = value + contract(flat_after[...], far[...])
    copy(total, influence)
    for each in copies:
        each.wait()


def per_device(gradients, targets):
    blocks, groups = lax.axis_size("blk"), lax.axis_size("tgt")
    rows, features = gradients.shape
    columns = targets.shape[1]
    half = rows // groups
    scale = 1.0 / (features * groups) ** 0.5
    forward = [(b, b - b % 4 + AFTER[b % 4]) for b in range(blocks)]
    back = [(b, b - b % 4 + BEFORE[b % 4]) for b in range(blocks)]
    across = [(t, 1 - t) for t in range(groups)]
    back_across = [(b * groups + t, c * groups + 1 - t) for b, c in back for t in range(groups)]

    def f32(*shape):
        return jax.ShapeDtypeStruct(shape, jnp.float32)

    def b16(*shape):
        return jax.ShapeDtypeStruct(shape, jnp.bfloat16)

    widths = [half * n // 16 for n in SIXTEENTHS]
    spans = [(sum(widths[:i]), w) for i, w in enumerate(widths)]
    first = spans[2][0]
    edge = half // 2
    flat = targets.T

    piece, mark = call(
        functools.partial(first_kernel, widths[0], half),
        [b16(2 * widths[0], features), f32(8, 128)],
        [ANY],
        [ANY, VMEM],
        [pltpu.SemaphoreType.DMA((2,))],
        vmem=FIRST_VMEM,
    )(gradients)
    gradients = call(
        load_kernel,
        b16(rows, features),
        [ANY] * 2,
        ANY,
        [pltpu.SemaphoreType.DMA((4,))],
        vmem=48,
    )(gradients, mark)
    sent, kept = call(
        functools.partial(self_kernel, half), [f32(half, rows)] * 2, [VMEM, ANY], [VMEM] * 2
    )(gradients, mark)
    pieces = call(
        functools.partial(rest_kernel, spans[1:], half),
        [b16(2 * w, features) for w in widths[1:]],
        [ANY] * 2,
        [ANY] * len(widths[1:]),
        [pltpu.SemaphoreType.DMA((2 * len(widths[1:]),))],
    )(gradients, kept)
    got = [lax.ppermute(piece, "blk", forward) for piece in (piece, *pieces)]
    self_tile = call(
        functools.partial(self_finish_kernel, scale), b16(half, rows), [VMEM] * 2, VMEM
    )(kept, lax.ppermute(sent, "tgt", across))

    def pair(width, piece, after):
        sent, kept = call(
            functools.partial(pair_kernel, width, half),
            [f32(3 * width, half)] * 2,
            [VMEM] * 2 + [ANY],
            [VMEM] * 2,
        )(piece, gradients, after)
        return [kept, lax.ppermute(sent, "tgt", across)]

    flat_before = lax.ppermute(flat, "blk", forward)
    sums = pair(widths[0], got[0], mark) + pair(widths[1], got[1], mark)
    third_sums = pair(widths[2], got[2], self_tile)
    early, back_early, flat_after = call(
        functools.partial(finish_kernel, widths[:2], half, scale),
        [b16(2 * first, half), b16(first, rows), b16(columns, rows)],
        [VMEM, ANY] + [VMEM] * 4,
        [VMEM] * 3,
    )(flat, third_sums[0], *sums)
    back_early = lax.ppermute(back_early, "blk", back)
    flat_after = lax.ppermute(flat_after, "blk", back)
    *_, second, width = widths
    sent, kept, near, cross, third = call(
        functools.partial(last_pair_kernel, width, half, scale),
        [f32(2 * width, half)] * 2
        + [f32(width + second, rows), f32(width, rows), b16(2 * second, half)],
        [VMEM] * 4 + [ANY],
        [VMEM] * 5,
    )(got[3], gradients, *third_sums, early)
    cross = lax.ppermute(cross, ("blk", "tgt"), back_across)
    near = lax.ppermute(near, "blk", back)
    sent = lax.ppermute(sent, "tgt", across)

    tiles, partial = call(
        functools.partial(most_kernel, half, edge),
        [b16(3, half, rows), f32(columns, half)],
        [VMEM] * 3,
        [ANY, VMEM],
        [pltpu.VMEM((2, half, edge), jnp.bfloat16), pltpu.SemaphoreType.DMA((3,))],
    )(self_tile, early, flat)
    tiles, influence = call(
        functools.partial(last_kernel, half, edge, scale),
        [b16(3, half, rows), f32(columns, half)],
        [ANY] + [VMEM] * 10,
        [ANY] * 2,
        [
            pltpu.VMEM((2, half, half - edge), jnp.bfloat16),
            pltpu.VMEM((half, rows), jnp.bfloat16),
            pltpu.VMEM((2, half - edge, half), jnp.bfloat16),
            pltpu.VMEM((columns, half), jnp.float32),
            pltpu.SemaphoreType.DMA((5,)),
        ],
        {0: 0},
    )(tiles, partial, early, third, back_early, flat_before, flat_after,
      kept, sent, near, cross)
    return tiles, influence.T


def solution(mesh):
    return jax.shard_map(
        per_device,
        mesh=mesh,
        in_specs=(P("blk", "tgt"), P("blk", None)),
        out_specs=(P(None, ("blk", "tgt"), None), P(("blk", "tgt"), None)),
        check_vma=False,
    )
```

```python
import functools

import jax
import jax.numpy as jnp
from jax import lax
from jax.experimental import pallas as pl
from jax.experimental.pallas import tpu as pltpu
from jax.sharding import PartitionSpec as P

AFTER = {0: 1, 1: 3, 3: 2, 2: 0}
BEFORE = {after: before for before, after in AFTER.items()}
SIXTEENTHS = (5, 4, 3, 2, 2)

FIRST_VMEM = 50
EARLY = 3
FLOPS = 3000000000
VMEM = pl.BlockSpec(memory_space=pltpu.VMEM)
ANY = pl.BlockSpec(memory_space=pl.ANY)


def call(kernel, out, in_specs, out_specs, scratch=(), aliases=None, vmem=16, flops=0):
    return pl.pallas_call(
        kernel,
        out_shape=out,
        in_specs=in_specs,
        out_specs=out_specs,
        scratch_shapes=scratch,
        input_output_aliases=aliases or {},
        cost_estimate=pl.CostEstimate(flops=flops, bytes_accessed=0, transcendentals=0),
        compiler_params=pltpu.CompilerParams(vmem_limit_bytes=vmem * 2**20),
    )


def contract(left, right):
    return lax.dot_general(
        left, right, (((1,), (1,)), ((), ())), preferred_element_type=jnp.float32
    )


def multiply(left, right):
    return jnp.dot(left, right, preferred_element_type=jnp.float32)


def contract_turned(left, right):
    return contract(right, left).T


def part_of(index, size):
    return pl.ds(pl.multiple_of(index * size, size), size)


def run_copies(copies, sems):
    copies = [pltpu.make_async_copy(*ends, sems.at[i]) for i, ends in enumerate(copies)]
    for copy in copies:
        copy.start()
    for copy in copies:
        copy.wait()


def first_kernel(width, half, grads, out, mark, sems):
    run_copies(
        [
            (grads.at[pl.ds(h * half, width)], out.at[pl.ds(h * width, width)])
            for h in range(2)
        ],
        sems,
    )
    mark[...] = jnp.zeros_like(mark)


def load_kernel(grads, before, out, sems):
    del before
    size = grads.shape[0] // 4
    run_copies([(grads.at[pl.ds(i * size, size)], out.at[pl.ds(i * size, size)]) for i in range(4)], sems)


def rest_kernel(spans, half, grads, before, *refs):
    del before
    *outs, sems = refs
    run_copies(
        [
            (grads.at[pl.ds(h * half + at, width)], out.at[pl.ds(h * width, width)])
            for (at, width), out in zip(spans, outs)
            for h in range(2)
        ],
        sems,
    )


def self_kernel(half, grads, before, sent, kept):
    del before
    t = lax.axis_index("tgt")
    sent[...] = contract(grads[part_of(1 - t, half), :], grads[...])
    kept[...] = contract(grads[part_of(t, half), :], grads[...])


def self_finish_kernel(scale, kept, got, tile):
    tile[...] = ((kept[...] + got[...]) * scale).astype(jnp.bfloat16)


def share(sent, kept, width):
    t = lax.axis_index("tgt")
    sent[2 * width :, :] = kept[part_of(1 - t, width), :]
    kept[2 * width :, :] = sent[part_of(t, width), :]


def pair_kernel(width, half, piece, grads, before, sent, kept):
    del before
    t = lax.axis_index("tgt")
    product = contract_turned if 2 * width <= 128 else contract
    sent[: 2 * width, :] = product(piece[...], grads[part_of(1 - t, half), :])
    kept[: 2 * width, :] = product(piece[...], grads[part_of(t, half), :])
    share(sent, kept, width)


def last_pair_kernel(
    width, half, scale, piece, grads, before, third, got, sent, kept, near, cross, tile, back
):
    t = lax.axis_index("tgt")
    sent[...] = contract_turned(piece[...], grads[part_of(1 - t, half), :])
    kept[...] = contract_turned(piece[...], grads[part_of(t, half), :])
    for to, index in ((near, t), (cross, 1 - t)):
        to[:, part_of(t, half)] = kept[part_of(index, width), :]
        to[:, part_of(1 - t, half)] = sent[part_of(index, width), :]
    finish_kernel([back.shape[0]], half, scale, before, third, got, tile, back)


def finish_kernel(widths, half, scale, before, *refs):
    del before
    *ins, tile, back = refs
    t = lax.axis_index("tgt")
    at, total = 0, sum(widths)
    for i, width in enumerate(widths):
        kept, got = ins[2 * i : 2 * i + 2]
        value = ((kept[...] + got[...]) * scale).astype(jnp.bfloat16)
        for h in range(2):
            tile[h * total + at : h * total + at + width, :] = value[h * width : (h + 1) * width]
        back[at : at + width, part_of(1 - t, half)] = value[2 * width :]
        at += width
    back[:, part_of(t, half)] = tile[part_of(t, total), :]


def early_finish_kernel(widths, half, scale, flat, before, *refs):
    *ins, tile, back = refs
    total = sum(widths)
    finish_kernel(widths, half, scale, before, *ins, tile, back.at[pl.ds(0, total)])
    back[total:, :] = flat[...]


def meets_far():
    place = lax.rem(lax.axis_index("blk"), 4)
    return (place == 0) | (place == 3)


def own_slot():
    return jnp.where(meets_far(), 2, 1)


def most_kernel(half, edge, self_tile, tile, flat, tiles, partial, turned, sems):
    slot = own_slot()
    whole = pltpu.make_async_copy(self_tile, tiles.at[0], sems.at[0])
    whole.start()
    partial[...] = contract(flat[...], self_tile[...])
    copies, size = [], tile.shape[0] // 2
    for h in range(2):
        part = tile[h * size : h * size + edge, :]
        turned[h] = part.T
        copies.append(
            pltpu.make_async_copy(
                turned.at[h], tiles.at[slot, :, pl.ds(h * half, edge)], sems.at[1 + h]
            )
        )
        copies[h].start()
    whole.wait()
    for copy in copies:
        copy.wait()


def last_kernel(
    half, edge, scale, before, got, cross, near, kept, partial, early, third, back_early,
    back_third, flat_before, near_new, near_back, tiles, influence, turned, far, late, total, sems,
):
    del before
    slot = own_slot()
    width = near.shape[0]
    first, second = early.shape[0] // 2, third.shape[0] // 2
    done = first + second
    copies = []

    def copy(source, target):
        copies.append(pltpu.make_async_copy(source, target, sems.at[len(copies)]))
        copies[-1].start()

    copy(back_early.at[pl.ds(0, first)], tiles.at[3 - slot, pl.ds(0, first)])
    far[first:done, :] = back_third[...]
    summed = ((near[...] + cross[...]) * scale).astype(jnp.bfloat16)
    far[done:, :] = jnp.where(meets_far(), near_back[...], summed)
    copy(
        far.at[pl.ds(first, second + width)], tiles.at[3 - slot, pl.ds(first, second + width)]
    )
    new = ((kept[...] + got[...]) * scale).astype(jnp.bfloat16)
    new = jnp.where(meets_far(), new, near_new[...])
    value = partial[...]
    for h in range(2):
        start = h * half
        late[h, : first - edge, :] = early[h * first + edge : (h + 1) * first, :]
        late[h, first - edge : done - edge, :] = third[h * second : (h + 1) * second, :]
        late[h, done - edge :, :] = new[h * width : (h + 1) * width]
        turned[h] = late[h].T
        copy(turned.at[h], tiles.at[slot, :, pl.ds(start + edge, half - edge)])
        value += multiply(
            flat_before[:, start : start + edge], early[h * first : h * first + edge, :]
        ) + multiply(flat_before[:, start + edge : start + half], late[h])
    far[:first, :] = back_early[:first, :]
    total[...] = value + contract(back_early[first:, :], far[...])
    copy(total, influence)
    for each in copies:
        each.wait()


def per_device(gradients, targets):
    blocks, groups = lax.axis_size("blk"), lax.axis_size("tgt")
    rows, features = gradients.shape
    columns = targets.shape[1]
    half = rows // groups
    scale = 1.0 / (features * groups) ** 0.5
    forward = [(b, b - b % 4 + AFTER[b % 4]) for b in range(blocks)]
    back = [(b, b - b % 4 + BEFORE[b % 4]) for b in range(blocks)]
    across = [(t, 1 - t) for t in range(groups)]
    beside = [(b, b ^ 1) for b in range(blocks)]
    back_across = [
        (b * groups + t, c * groups + (1 - t if b % 4 in (0, 3) else t))
        for b, c in back
        for t in range(groups)
    ]

    def f32(*shape):
        return jax.ShapeDtypeStruct(shape, jnp.float32)

    def b16(*shape):
        return jax.ShapeDtypeStruct(shape, jnp.bfloat16)

    widths = [half * n // 16 for n in SIXTEENTHS]
    spans = [(sum(widths[:i]), w) for i, w in enumerate(widths)]
    first = spans[-2][0]
    edge = half // 2
    flat = targets.T

    piece, mark = call(
        functools.partial(first_kernel, widths[0], half),
        [b16(2 * widths[0], features), f32(8, 128)],
        [ANY],
        [ANY, VMEM],
        [pltpu.SemaphoreType.DMA((2,))],
        vmem=FIRST_VMEM,
    )(gradients)
    gradients = call(
        load_kernel,
        b16(rows, features),
        [ANY] * 2,
        ANY,
        [pltpu.SemaphoreType.DMA((4,))],
        vmem=48,
    )(gradients, mark)
    sent, kept = call(
        functools.partial(self_kernel, half), [f32(half, rows)] * 2, [VMEM, ANY], [VMEM] * 2
    )(gradients, mark)
    pieces = call(
        functools.partial(rest_kernel, spans[1:], half),
        [b16(2 * w, features) for w in widths[1:]],
        [ANY] * 2,
        [ANY] * len(widths[1:]),
        [pltpu.SemaphoreType.DMA((2 * len(widths[1:]),))],
    )(gradients, kept)
    got = [lax.ppermute(piece, "blk", forward) for piece in (piece, *pieces)]
    self_tile = call(
        functools.partial(self_finish_kernel, scale), b16(half, rows), [VMEM] * 2, VMEM
    )(kept, lax.ppermute(sent, "tgt", across))

    def pair(width, piece, after):
        sent, kept = call(
            functools.partial(pair_kernel, width, half),
            [f32(3 * width, half)] * 2,
            [VMEM] * 2 + [ANY],
            [VMEM] * 2,
        )(piece, gradients, after)
        return [kept, lax.ppermute(sent, "tgt", across)]

    flat_before = lax.ppermute(flat, "blk", forward)
    near_sums = pair(widths[-1], lax.ppermute(pieces[-1], "blk", beside), mark)
    near_new, near_back = call(
        functools.partial(finish_kernel, widths[-1:], half, scale),
        [b16(2 * widths[-1], half), b16(widths[-1], rows)],
        [ANY] + [VMEM] * 2,
        [VMEM] * 2,
    )(mark, *near_sums)
    near_back = lax.ppermute(near_back, "blk", beside)
    sums = pair(widths[0], got[0], near_back)
    for w, piece in zip(widths[1:-2], got[1:-2]):
        sums += pair(w, piece, mark)
    sums += pair(widths[-2], got[-2], self_tile)

    some = widths[:EARLY]
    early, back_early = call(
        functools.partial(early_finish_kernel, some, half, scale),
        [b16(2 * sum(some), half), b16(sum(some) + columns, rows)],
        [VMEM, ANY] + [VMEM] * (2 * EARLY),
        [VMEM] * 2,
    )(flat, sums[-2], *sums[: 2 * EARLY])
    back_early = lax.ppermute(back_early, "blk", back)
    *_, second, width = widths
    sent, kept, near, cross, third, back_third = call(
        functools.partial(last_pair_kernel, width, half, scale),
        [f32(2 * width, half)] * 2
        + [f32(width, rows)] * 2
        + [b16(2 * second, half), b16(second, rows)],
        [VMEM] * 2 + [ANY] + [VMEM] * 2,
        [VMEM] * 6,
        flops=FLOPS,
    )(got[-1], gradients, early, *sums[2 * EARLY :])
    sent = lax.ppermute(sent, "tgt", across)
    near = lax.ppermute(near, "blk", back)
    cross = lax.ppermute(cross, ("blk", "tgt"), back_across)
    back_third = lax.ppermute(back_third, "blk", back)

    tiles, partial = call(
        functools.partial(most_kernel, half, edge),
        [b16(3, half, rows), f32(columns, half)],
        [VMEM] * 3,
        [ANY, VMEM],
        [pltpu.VMEM((2, half, edge), jnp.bfloat16), pltpu.SemaphoreType.DMA((3,))],
    )(self_tile, early, flat)
    tiles, influence = call(
        functools.partial(last_kernel, half, edge, scale),
        [b16(3, half, rows), f32(columns, half)],
        [ANY] + [VMEM] * 12,
        [ANY] * 2,
        [
            pltpu.VMEM((2, half, half - edge), jnp.bfloat16),
            pltpu.VMEM((half, rows), jnp.bfloat16),
            pltpu.VMEM((2, half - edge, half), jnp.bfloat16),
            pltpu.VMEM((columns, half), jnp.float32),
            pltpu.SemaphoreType.DMA((5,)),
        ],
        {0: 0},
    )(
        tiles, sent, cross, near, kept, partial, early, third, back_early, back_third,
        flat_before, near_new, near_back,
    )
    return tiles, influence.T


def solution(mesh):
    return jax.shard_map(
        per_device,
        mesh=mesh,
        in_specs=(P("blk", "tgt"), P("blk", None)),
        out_specs=(P(None, ("blk", "tgt"), None), P(("blk", "tgt"), None)),
        check_vma=False,
    )
```

```python
import functools

import jax
import jax.numpy as jnp
from jax import lax
from jax.experimental import pallas as pl
from jax.experimental.pallas import tpu as pltpu
from jax.sharding import PartitionSpec as P

AFTER = {0: 1, 1: 3, 3: 2, 2: 0}
BEFORE = {after: before for before, after in AFTER.items()}
SIXTEENTHS = (5, 4, 3, 2, 2)

FIRST_VMEM = 50
EARLY = 3
FLOPS = 1500000000
VMEM = pl.BlockSpec(memory_space=pltpu.VMEM)
ANY = pl.BlockSpec(memory_space=pl.ANY)


def call(kernel, out, in_specs, out_specs, scratch=(), aliases=None, vmem=16, flops=0):
    return pl.pallas_call(
        kernel,
        out_shape=out,
        in_specs=in_specs,
        out_specs=out_specs,
        scratch_shapes=scratch,
        input_output_aliases=aliases or {},
        cost_estimate=pl.CostEstimate(flops=flops, bytes_accessed=0, transcendentals=0),
        compiler_params=pltpu.CompilerParams(vmem_limit_bytes=vmem * 2**20),
    )


def contract(left, right):
    return lax.dot_general(
        left, right, (((1,), (1,)), ((), ())), preferred_element_type=jnp.float32
    )


def multiply(left, right):
    return jnp.dot(left, right, preferred_element_type=jnp.float32)


def contract_turned(left, right):
    return contract(right, left).T


def part_of(index, size):
    return pl.ds(pl.multiple_of(index * size, size), size)


def run_copies(copies, sems):
    copies = [pltpu.make_async_copy(*ends, sems.at[i]) for i, ends in enumerate(copies)]
    for copy in copies:
        copy.start()
    for copy in copies:
        copy.wait()


def first_kernel(width, half, grads, out, mark, sems):
    run_copies(
        [
            (grads.at[pl.ds(h * half, width)], out.at[pl.ds(h * width, width)])
            for h in range(2)
        ],
        sems,
    )
    mark[...] = jnp.zeros_like(mark)


def load_kernel(grads, before, out, sems):
    del before
    size = grads.shape[0] // 4
    run_copies([(grads.at[pl.ds(i * size, size)], out.at[pl.ds(i * size, size)]) for i in range(4)], sems)


def rest_kernel(spans, half, grads, before, *refs):
    del before
    *outs, sems = refs
    run_copies(
        [
            (grads.at[pl.ds(h * half + at, width)], out.at[pl.ds(h * width, width)])
            for (at, width), out in zip(spans, outs)
            for h in range(2)
        ],
        sems,
    )


def self_kernel(half, grads, before, sent, kept):
    del before
    t = lax.axis_index("tgt")
    sent[...] = contract(grads[part_of(1 - t, half), :], grads[...])
    kept[...] = contract(grads[part_of(t, half), :], grads[...])


def self_finish_kernel(scale, kept, got, tile):
    tile[...] = ((kept[...] + got[...]) * scale).astype(jnp.bfloat16)


def share(sent, kept, width):
    t = lax.axis_index("tgt")
    sent[2 * width :, :] = kept[part_of(1 - t, width), :]
    kept[2 * width :, :] = sent[part_of(t, width), :]


def pair_kernel(width, half, piece, grads, before, sent, kept):
    del before
    t = lax.axis_index("tgt")
    product = contract_turned if 2 * width <= 128 else contract
    sent[: 2 * width, :] = product(piece[...], grads[part_of(1 - t, half), :])
    kept[: 2 * width, :] = product(piece[...], grads[part_of(t, half), :])
    share(sent, kept, width)


def last_pair_kernel(
    width, half, scale, piece, grads, before, third, got, sent, kept, near, cross, tile, back
):
    @pl.when(meets_far())
    def _():
        t = lax.axis_index("tgt")
        sent[...] = contract_turned(piece[...], grads[part_of(1 - t, half), :])
        kept[...] = contract_turned(piece[...], grads[part_of(t, half), :])
        for to, index in ((near, t), (cross, 1 - t)):
            to[:, part_of(t, half)] = kept[part_of(index, width), :]
            to[:, part_of(1 - t, half)] = sent[part_of(index, width), :]

    finish_kernel([back.shape[0]], half, scale, before, third, got, tile, back)


def finish_kernel(widths, half, scale, before, *refs):
    del before
    *ins, tile, back = refs
    t = lax.axis_index("tgt")
    at, total = 0, sum(widths)
    for i, width in enumerate(widths):
        kept, got = ins[2 * i : 2 * i + 2]
        value = ((kept[...] + got[...]) * scale).astype(jnp.bfloat16)
        for h in range(2):
            tile[h * total + at : h * total + at + width, :] = value[h * width : (h + 1) * width]
        back[at : at + width, part_of(1 - t, half)] = value[2 * width :]
        at += width
    back[:, part_of(t, half)] = tile[part_of(t, total), :]


def early_finish_kernel(widths, half, scale, flat, before, *refs):
    *ins, tile, back = refs
    total = sum(widths)
    finish_kernel(widths, half, scale, before, *ins, tile, back.at[pl.ds(0, total)])
    back[total:, :] = flat[...]


def meets_far():
    place = lax.rem(lax.axis_index("blk"), 4)
    return (place == 0) | (place == 3)


def own_slot():
    return jnp.where(meets_far(), 2, 1)


def most_kernel(half, edge, self_tile, tile, flat, tiles, partial, turned, sems):
    slot = own_slot()
    whole = pltpu.make_async_copy(self_tile, tiles.at[0], sems.at[0])
    whole.start()
    partial[...] = contract(flat[...], self_tile[...])
    copies, size = [], tile.shape[0] // 2
    for h in range(2):
        part = tile[h * size : h * size + edge, :]
        turned[h] = part.T
        copies.append(
            pltpu.make_async_copy(
                turned.at[h], tiles.at[slot, :, pl.ds(h * half, edge)], sems.at[1 + h]
            )
        )
        copies[h].start()
    whole.wait()
    for copy in copies:
        copy.wait()


def last_kernel(
    half, edge, scale, before, cross, got, near, kept, partial, early, third, back_early,
    back_third, flat_before, near_new, near_back, tiles, influence, turned, far, late, total, sems,
):
    del before
    slot = own_slot()
    width = near.shape[0]
    first, second = early.shape[0] // 2, third.shape[0] // 2
    done = first + second
    copies = []

    def copy(source, target):
        copies.append(pltpu.make_async_copy(source, target, sems.at[len(copies)]))
        copies[-1].start()

    copy(back_early.at[pl.ds(0, first)], tiles.at[3 - slot, pl.ds(0, first)])
    far[first:done, :] = back_third[...]
    summed = ((near[...] + cross[...]) * scale).astype(jnp.bfloat16)
    far[done:, :] = jnp.where(meets_far(), near_back[...], summed)
    copy(
        far.at[pl.ds(first, second + width)], tiles.at[3 - slot, pl.ds(first, second + width)]
    )
    new = ((kept[...] + got[...]) * scale).astype(jnp.bfloat16)
    new = jnp.where(meets_far(), new, near_new[...])
    value = partial[...]
    for h in range(2):
        start = h * half
        late[h, : first - edge, :] = early[h * first + edge : (h + 1) * first, :]
        late[h, first - edge : done - edge, :] = third[h * second : (h + 1) * second, :]
        late[h, done - edge :, :] = new[h * width : (h + 1) * width]
        turned[h] = late[h].T
        copy(turned.at[h], tiles.at[slot, :, pl.ds(start + edge, half - edge)])
        value += multiply(
            flat_before[:, start : start + edge], early[h * first : h * first + edge, :]
        ) + multiply(flat_before[:, start + edge : start + half], late[h])
    far[:first, :] = back_early[:first, :]
    total[...] = value + contract(back_early[first:, :], far[...])
    copy(total, influence)
    for each in copies:
        each.wait()


def per_device(gradients, targets):
    blocks, groups = lax.axis_size("blk"), lax.axis_size("tgt")
    rows, features = gradients.shape
    columns = targets.shape[1]
    half = rows // groups
    scale = 1.0 / (features * groups) ** 0.5
    forward = [(b, b - b % 4 + AFTER[b % 4]) for b in range(blocks)]
    back = [(b, b - b % 4 + BEFORE[b % 4]) for b in range(blocks)]
    across = [(t, 1 - t) for t in range(groups)]
    beside = [(b, b ^ 1) for b in range(blocks)]
    back_across = [
        (b * groups + t, c * groups + (1 - t if b % 4 in (0, 3) else t))
        for b, c in back
        for t in range(groups)
    ]

    def f32(*shape):
        return jax.ShapeDtypeStruct(shape, jnp.float32)

    def b16(*shape):
        return jax.ShapeDtypeStruct(shape, jnp.bfloat16)

    widths = [half * n // 16 for n in SIXTEENTHS]
    spans = [(sum(widths[:i]), w) for i, w in enumerate(widths)]
    first = spans[-2][0]
    edge = half // 2
    flat = targets.T

    piece, mark = call(
        functools.partial(first_kernel, widths[0], half),
        [b16(2 * widths[0], features), f32(8, 128)],
        [ANY],
        [ANY, VMEM],
        [pltpu.SemaphoreType.DMA((2,))],
        vmem=FIRST_VMEM,
    )(gradients)
    gradients = call(
        load_kernel,
        b16(rows, features),
        [ANY] * 2,
        ANY,
        [pltpu.SemaphoreType.DMA((4,))],
        vmem=48,
    )(gradients, mark)
    sent, kept = call(
        functools.partial(self_kernel, half), [f32(half, rows)] * 2, [VMEM, ANY], [VMEM] * 2
    )(gradients, mark)
    pieces = call(
        functools.partial(rest_kernel, spans[1:], half),
        [b16(2 * w, features) for w in widths[1:]],
        [ANY] * 2,
        [ANY] * len(widths[1:]),
        [pltpu.SemaphoreType.DMA((2 * len(widths[1:]),))],
    )(gradients, kept)
    got = [lax.ppermute(piece, "blk", forward) for piece in (piece, *pieces)]
    self_tile = call(
        functools.partial(self_finish_kernel, scale), b16(half, rows), [VMEM] * 2, VMEM
    )(kept, lax.ppermute(sent, "tgt", across))

    def pair(width, piece, after):
        sent, kept = call(
            functools.partial(pair_kernel, width, half),
            [f32(3 * width, half)] * 2,
            [VMEM] * 2 + [ANY],
            [VMEM] * 2,
        )(piece, gradients, after)
        return [kept, lax.ppermute(sent, "tgt", across)]

    flat_before = lax.ppermute(flat, "blk", forward)
    near_sums = pair(widths[-1], lax.ppermute(pieces[-1], "blk", beside), mark)
    near_new, near_back = call(
        functools.partial(finish_kernel, widths[-1:], half, scale),
        [b16(2 * widths[-1], half), b16(widths[-1], rows)],
        [ANY] + [VMEM] * 2,
        [VMEM] * 2,
    )(mark, *near_sums)
    near_back = lax.ppermute(near_back, "blk", beside)
    sums = pair(widths[0], got[0], near_back)
    for w, piece in zip(widths[1:-2], got[1:-2]):
        sums += pair(w, piece, mark)
    sums += pair(widths[-2], got[-2], self_tile)

    some = widths[:EARLY]
    early, back_early = call(
        functools.partial(early_finish_kernel, some, half, scale),
        [b16(2 * sum(some), half), b16(sum(some) + columns, rows)],
        [VMEM, ANY] + [VMEM] * (2 * EARLY),
        [VMEM] * 2,
    )(flat, sums[-2], *sums[: 2 * EARLY])
    back_early = lax.ppermute(back_early, "blk", back)
    *_, second, width = widths
    sent, kept, near, cross, third, back_third = call(
        functools.partial(last_pair_kernel, width, half, scale),
        [f32(2 * width, half)] * 2
        + [f32(width, rows)] * 2
        + [b16(2 * second, half), b16(second, rows)],
        [VMEM] * 2 + [ANY] + [VMEM] * 2,
        [VMEM] * 6,
        flops=FLOPS,
    )(got[-1], gradients, early, *sums[2 * EARLY :])
    sent = lax.ppermute(sent, "tgt", across)
    near = lax.ppermute(near, "blk", back)
    cross = lax.ppermute(cross, ("blk", "tgt"), back_across)
    back_third = lax.ppermute(back_third, "blk", back)

    tiles, partial = call(
        functools.partial(most_kernel, half, edge),
        [b16(3, half, rows), f32(columns, half)],
        [VMEM] * 3,
        [ANY, VMEM],
        [pltpu.VMEM((2, half, edge), jnp.bfloat16), pltpu.SemaphoreType.DMA((3,))],
    )(self_tile, early, flat)
    tiles, influence = call(
        functools.partial(last_kernel, half, edge, scale),
        [b16(3, half, rows), f32(columns, half)],
        [ANY] + [VMEM] * 12,
        [ANY] * 2,
        [
            pltpu.VMEM((2, half, half - edge), jnp.bfloat16),
            pltpu.VMEM((half, rows), jnp.bfloat16),
            pltpu.VMEM((2, half - edge, half), jnp.bfloat16),
            pltpu.VMEM((columns, half), jnp.float32),
            pltpu.SemaphoreType.DMA((5,)),
        ],
        {0: 0},
    )(
        tiles, cross, sent, near, kept, partial, early, third, back_early, back_third,
        flat_before, near_new, near_back,
    )
    return tiles, influence.T


def solution(mesh):
    return jax.shard_map(
        per_device,
        mesh=mesh,
        in_specs=(P("blk", "tgt"), P("blk", None)),
        out_specs=(P(None, ("blk", "tgt"), None), P(("blk", "tgt"), None)),
        check_vma=False,
    )
```

```python
import functools

import jax
import jax.numpy as jnp
from jax import lax
from jax.experimental import pallas as pl
from jax.experimental.pallas import tpu as pltpu
from jax.sharding import PartitionSpec as P

AFTER = {0: 1, 1: 3, 3: 2, 2: 0}
BEFORE = {after: before for before, after in AFTER.items()}
SIXTEENTHS = (5, 4, 3, 2, 2)
EARLY = 3
FIRST_VMEM = 50
FLOPS = 3000000000
VMEM = pl.BlockSpec(memory_space=pltpu.VMEM)
ANY = pl.BlockSpec(memory_space=pl.ANY)


def call(kernel, out, in_specs, out_specs, scratch=(), aliases=None, vmem=16, flops=0):
    return pl.pallas_call(
        kernel,
        out_shape=out,
        in_specs=in_specs,
        out_specs=out_specs,
        scratch_shapes=scratch,
        input_output_aliases=aliases or {},
        cost_estimate=pl.CostEstimate(flops=flops, bytes_accessed=0, transcendentals=0),
        compiler_params=pltpu.CompilerParams(vmem_limit_bytes=vmem * 2**20),
    )


def contract(left, right):
    return lax.dot_general(
        left, right, (((1,), (1,)), ((), ())), preferred_element_type=jnp.float32
    )


def multiply(left, right):
    return jnp.dot(left, right, preferred_element_type=jnp.float32)


def contract_turned(left, right):
    return contract(right, left).T


def part_of(index, size):
    return pl.ds(pl.multiple_of(index * size, size), size)


def run_copies(copies, sems):
    copies = [pltpu.make_async_copy(*ends, sems.at[i]) for i, ends in enumerate(copies)]
    for copy in copies:
        copy.start()
    for copy in copies:
        copy.wait()


def first_kernel(width, half, grads, out, mark, sems):
    run_copies(
        [
            (grads.at[pl.ds(h * half, width)], out.at[pl.ds(h * width, width)])
            for h in range(2)
        ],
        sems,
    )
    mark[...] = jnp.zeros_like(mark)


def load_kernel(grads, before, out, sems):
    del before
    size = grads.shape[0] // 4
    parts = [pl.ds(i * size, size) for i in range(4)]
    run_copies([(grads.at[part], out.at[part]) for part in parts], sems)


def rest_kernel(spans, half, grads, before, *refs):
    del before
    *outs, sems = refs
    run_copies(
        [
            (grads.at[pl.ds(h * half + at, width)], out.at[pl.ds(h * width, width)])
            for (at, width), out in zip(spans, outs)
            for h in range(2)
        ],
        sems,
    )


def self_kernel(half, grads, before, sent, kept):
    del before
    t = lax.axis_index("tgt")
    sent[...] = contract(grads[part_of(1 - t, half), :], grads[...])
    kept[...] = contract(grads[part_of(t, half), :], grads[...])


def self_finish_kernel(scale, kept, got, tile):
    tile[...] = ((kept[...] + got[...]) * scale).astype(jnp.bfloat16)


def share(sent, kept, width):
    t = lax.axis_index("tgt")
    sent[2 * width :, :] = kept[part_of(1 - t, width), :]
    kept[2 * width :, :] = sent[part_of(t, width), :]


def pair_kernel(width, half, piece, grads, before, sent, kept):
    del before
    t = lax.axis_index("tgt")
    product = contract_turned if 2 * width <= 128 else contract
    sent[: 2 * width, :] = product(piece[...], grads[part_of(1 - t, half), :])
    kept[: 2 * width, :] = product(piece[...], grads[part_of(t, half), :])
    share(sent, kept, width)


def last_pair_kernel(width, half, piece, grads, before, sent, kept, near, cross):
    del before

    @pl.when(meets_far())
    def _():
        t = lax.axis_index("tgt")
        sent[...] = contract_turned(piece[...], grads[part_of(1 - t, half), :])
        kept[...] = contract_turned(piece[...], grads[part_of(t, half), :])
        for to, index in ((near, t), (cross, 1 - t)):
            to[:, part_of(t, half)] = kept[part_of(index, width), :]
            to[:, part_of(1 - t, half)] = sent[part_of(index, width), :]


def hand_on_kernel(half, scale, third, got, sent, near, cross, tile, back, *outs):
    finish_kernel([back.shape[0]], half, scale, None, third, got, tile, back)
    for value, out in zip((sent, near, cross), outs):
        out[...] = value[...]


def finish_kernel(widths, half, scale, before, *refs):
    del before
    *ins, tile, back = refs
    t = lax.axis_index("tgt")
    at, total = 0, sum(widths)
    for i, width in enumerate(widths):
        kept, got = ins[2 * i : 2 * i + 2]
        value = ((kept[...] + got[...]) * scale).astype(jnp.bfloat16)
        for h in range(2):
            tile[h * total + at : h * total + at + width, :] = value[h * width : (h + 1) * width]
        back[at : at + width, part_of(1 - t, half)] = value[2 * width :]
        at += width
    back[:, part_of(t, half)] = tile[part_of(t, total), :]


def early_finish_kernel(widths, half, scale, flat, before, *refs):
    *ins, tile, back = refs
    total = sum(widths)
    finish_kernel(widths, half, scale, before, *ins, tile, back.at[pl.ds(0, total)])
    back[total:, :] = flat[...]


def meets_far():
    place = lax.rem(lax.axis_index("blk"), 4)
    return (place == 0) | (place == 3)


def own_slot():
    return jnp.where(meets_far(), 2, 1)


def most_kernel(half, edge, self_tile, tile, flat, tiles, partial, turned, sems):
    slot = own_slot()
    whole = pltpu.make_async_copy(self_tile, tiles.at[0], sems.at[0])
    whole.start()
    partial[...] = contract(flat[...], self_tile[...])
    copies, size = [], tile.shape[0] // 2
    for h in range(2):
        part = tile[h * size : h * size + edge, :]
        turned[h] = part.T
        copies.append(
            pltpu.make_async_copy(
                turned.at[h], tiles.at[slot, :, pl.ds(h * half, edge)], sems.at[1 + h]
            )
        )
        copies[h].start()
    whole.wait()
    for copy in copies:
        copy.wait()


def last_kernel(
    half, edge, scale, before, got, cross, near, kept, partial, early, third, back_early,
    back_third, flat_before, near_new, near_back, tiles, influence, turned, far, late, total, sems,
):
    del before
    slot = own_slot()
    width = near.shape[0]
    first, second = early.shape[0] // 2, third.shape[0] // 2
    done = first + second
    copies = []

    def copy(source, target):
        copies.append(pltpu.make_async_copy(source, target, sems.at[len(copies)]))
        copies[-1].start()

    copy(back_early.at[pl.ds(0, first)], tiles.at[3 - slot, pl.ds(0, first)])
    far[first:done, :] = back_third[...]
    summed = ((near[...] + cross[...]) * scale).astype(jnp.bfloat16)
    far[done:, :] = jnp.where(meets_far(), near_back[...], summed)
    copy(
        far.at[pl.ds(first, second + width)], tiles.at[3 - slot, pl.ds(first, second + width)]
    )
    new = ((kept[...] + got[...]) * scale).astype(jnp.bfloat16)
    new = jnp.where(meets_far(), new, near_new[...])
    value = partial[...]
    for h in range(2):
        start = h * half
        late[h, : first - edge, :] = early[h * first + edge : (h + 1) * first, :]
        late[h, first - edge : done - edge, :] = third[h * second : (h + 1) * second, :]
        late[h, done - edge :, :] = new[h * width : (h + 1) * width]
        turned[h] = late[h].T
        copy(turned.at[h], tiles.at[slot, :, pl.ds(start + edge, half - edge)])
        value += multiply(
            flat_before[:, start : start + edge], early[h * first : h * first + edge, :]
        ) + multiply(flat_before[:, start + edge : start + half], late[h])
    far[:first, :] = back_early[:first, :]
    total[...] = value + contract(back_early[first:, :], far[...])
    copy(total, influence)
    for each in copies:
        each.wait()


def per_device(gradients, targets):
    blocks, groups = lax.axis_size("blk"), lax.axis_size("tgt")
    rows, features = gradients.shape
    columns = targets.shape[1]
    half = rows // groups
    scale = 1.0 / (features * groups) ** 0.5
    forward = [(b, b - b % 4 + AFTER[b % 4]) for b in range(blocks)]
    back = [(b, b - b % 4 + BEFORE[b % 4]) for b in range(blocks)]
    across = [(t, 1 - t) for t in range(groups)]
    beside = [(b, b ^ 1) for b in range(blocks)]
    back_across = [
        (b * groups + t, c * groups + (1 - t if b % 4 in (0, 3) else t))
        for b, c in back
        for t in range(groups)
    ]

    def f32(*shape):
        return jax.ShapeDtypeStruct(shape, jnp.float32)

    def b16(*shape):
        return jax.ShapeDtypeStruct(shape, jnp.bfloat16)

    widths = [half * n // 16 for n in SIXTEENTHS]
    spans = [(sum(widths[:i]), w) for i, w in enumerate(widths)]
    first = spans[-2][0]
    edge = half // 2
    flat = targets.T

    piece, mark = call(
        functools.partial(first_kernel, widths[0], half),
        [b16(2 * widths[0], features), f32(8, 128)],
        [ANY],
        [ANY, VMEM],
        [pltpu.SemaphoreType.DMA((2,))],
        vmem=FIRST_VMEM,
    )(gradients)
    gradients = call(
        load_kernel,
        b16(rows, features),
        [ANY] * 2,
        ANY,
        [pltpu.SemaphoreType.DMA((4,))],
        vmem=48,
    )(gradients, mark)
    sent, kept = call(
        functools.partial(self_kernel, half), [f32(half, rows)] * 2, [VMEM, ANY], [VMEM] * 2
    )(gradients, mark)
    pieces = call(
        functools.partial(rest_kernel, spans[1:], half),
        [b16(2 * w, features) for w in widths[1:]],
        [ANY] * 2,
        [ANY] * len(widths[1:]),
        [pltpu.SemaphoreType.DMA((2 * len(widths[1:]),))],
    )(gradients, kept)
    got = [lax.ppermute(piece, "blk", forward) for piece in (piece, *pieces)]
    self_tile = call(
        functools.partial(self_finish_kernel, scale), b16(half, rows), [VMEM] * 2, VMEM
    )(kept, lax.ppermute(sent, "tgt", across))

    def pair(width, piece, after):
        sent, kept = call(
            functools.partial(pair_kernel, width, half),
            [f32(3 * width, half)] * 2,
            [VMEM] * 2 + [ANY],
            [VMEM] * 2,
        )(piece, gradients, after)
        return [kept, lax.ppermute(sent, "tgt", across)]

    flat_before = lax.ppermute(flat, "blk", forward)
    near_sums = pair(widths[-1], lax.ppermute(pieces[-1], "blk", beside), mark)
    near_new, near_back = call(
        functools.partial(finish_kernel, widths[-1:], half, scale),
        [b16(2 * widths[-1], half), b16(widths[-1], rows)],
        [ANY] + [VMEM] * 2,
        [VMEM] * 2,
    )(mark, *near_sums)
    near_back = lax.ppermute(near_back, "blk", beside)
    sums = pair(widths[0], got[0], near_back)
    for w, piece in zip(widths[1:-2], got[1:-2]):
        sums += pair(w, piece, mark)
    sums += pair(widths[-2], got[-2], self_tile)

    some = widths[:EARLY]
    early, back_early = call(
        functools.partial(early_finish_kernel, some, half, scale),
        [b16(2 * sum(some), half), b16(sum(some) + columns, rows)],
        [VMEM, ANY] + [VMEM] * (2 * EARLY),
        [VMEM] * 2,
    )(flat, sums[-2], *sums[: 2 * EARLY])
    back_early = lax.ppermute(back_early, "blk", back)
    *_, second, width = widths
    shapes = [f32(2 * width, half)] + [f32(width, rows)] * 2
    sent, kept, near, cross = call(
        functools.partial(last_pair_kernel, width, half),
        [shapes[0], *shapes],
        [VMEM] * 2 + [ANY],
        [VMEM] * 4,
    )(got[-1], gradients, early)
    third, back_third, sent, near, cross = call(
        functools.partial(hand_on_kernel, half, scale),
        [b16(2 * second, half), b16(second, rows), *shapes],
        [VMEM] * 5,
        [VMEM] * 5,
        flops=FLOPS,
    )(*sums[2 * EARLY :], sent, near, cross)
    sent = lax.ppermute(sent, "tgt", across)
    near = lax.ppermute(near, "blk", back)
    cross = lax.ppermute(cross, ("blk", "tgt"), back_across)
    back_third = lax.ppermute(back_third, "blk", back)

    tiles, partial = call(
        functools.partial(most_kernel, half, edge),
        [b16(3, half, rows), f32(columns, half)],
        [VMEM] * 3,
        [ANY, VMEM],
        [pltpu.VMEM((2, half, edge), jnp.bfloat16), pltpu.SemaphoreType.DMA((3,))],
    )(self_tile, early, flat)
    tiles, influence = call(
        functools.partial(last_kernel, half, edge, scale),
        [b16(3, half, rows), f32(columns, half)],
        [ANY] + [VMEM] * 12,
        [ANY] * 2,
        [
            pltpu.VMEM((2, half, half - edge), jnp.bfloat16),
            pltpu.VMEM((half, rows), jnp.bfloat16),
            pltpu.VMEM((2, half - edge, half), jnp.bfloat16),
            pltpu.VMEM((columns, half), jnp.float32),
            pltpu.SemaphoreType.DMA((5,)),
        ],
        {0: 0},
    )(
        tiles, sent, cross, near, kept, partial, early, third, back_early, back_third,
        flat_before, near_new, near_back,
    )
    return tiles, influence.T


def solution(mesh):
    return jax.shard_map(
        per_device,
        mesh=mesh,
        in_specs=(P("blk", "tgt"), P("blk", None)),
        out_specs=(P(None, ("blk", "tgt"), None), P(("blk", "tgt"), None)),
        check_vma=False,
    )
```

```python
import functools

import jax
import jax.numpy as jnp
from jax import lax
from jax.experimental import pallas as pl
from jax.experimental.pallas import tpu as pltpu
from jax.sharding import PartitionSpec as P

AFTER = {0: 1, 1: 3, 3: 2, 2: 0}
BEFORE = {after: before for before, after in AFTER.items()}
SIXTEENTHS = (5, 4, 3, 2, 2)
EARLY = 3
FIRST_VMEM = 50
FLOPS = 3000000000
VMEM = pl.BlockSpec(memory_space=pltpu.VMEM)
ANY = pl.BlockSpec(memory_space=pl.ANY)


def call(kernel, out, in_specs, out_specs, scratch=(), aliases=None, vmem=16, flops=0):
    return pl.pallas_call(
        kernel,
        out_shape=out,
        in_specs=in_specs,
        out_specs=out_specs,
        scratch_shapes=scratch,
        input_output_aliases=aliases or {},
        cost_estimate=pl.CostEstimate(flops=flops, bytes_accessed=0, transcendentals=0),
        compiler_params=pltpu.CompilerParams(vmem_limit_bytes=vmem * 2**20),
    )


def contract(left, right):
    return lax.dot_general(
        left, right, (((1,), (1,)), ((), ())), preferred_element_type=jnp.float32
    )


def multiply(left, right):
    return jnp.dot(left, right, preferred_element_type=jnp.float32)


def contract_turned(left, right):
    return contract(right, left).T


def part_of(index, size):
    return pl.ds(pl.multiple_of(index * size, size), size)


def run_copies(copies, sems):
    copies = [pltpu.make_async_copy(*ends, sems.at[i]) for i, ends in enumerate(copies)]
    for copy in copies:
        copy.start()
    for copy in copies:
        copy.wait()


def first_kernel(width, half, grads, out, mark, sems):
    run_copies(
        [
            (grads.at[pl.ds(h * half, width)], out.at[pl.ds(h * width, width)])
            for h in range(2)
        ],
        sems,
    )
    mark[...] = jnp.zeros_like(mark)


def load_kernel(grads, before, out, sems):
    del before
    size = grads.shape[0] // 4
    parts = [pl.ds(i * size, size) for i in range(4)]
    run_copies([(grads.at[part], out.at[part]) for part in parts], sems)


def rest_kernel(spans, half, grads, before, *refs):
    del before
    *outs, sems = refs
    run_copies(
        [
            (grads.at[pl.ds(h * half + at, width)], out.at[pl.ds(h * width, width)])
            for (at, width), out in zip(spans, outs)
            for h in range(2)
        ],
        sems,
    )


def self_kernel(half, grads, before, sent, kept):
    del before
    t = lax.axis_index("tgt")
    sent[...] = contract(grads[part_of(1 - t, half), :], grads[...])
    kept[...] = contract(grads[part_of(t, half), :], grads[...])


def self_finish_kernel(scale, kept, got, tile):
    tile[...] = ((kept[...] + got[...]) * scale).astype(jnp.bfloat16)


def share(sent, kept, width):
    t = lax.axis_index("tgt")
    sent[2 * width :, :] = kept[part_of(1 - t, width), :]
    kept[2 * width :, :] = sent[part_of(t, width), :]


def pair_kernel(width, half, piece, grads, before, sent, kept):
    del before
    t = lax.axis_index("tgt")
    product = contract_turned if 2 * width <= 128 else contract
    sent[: 2 * width, :] = product(piece[...], grads[part_of(1 - t, half), :])
    kept[: 2 * width, :] = product(piece[...], grads[part_of(t, half), :])
    share(sent, kept, width)


def last_pair_kernel(width, half, piece, grads, before, sent, kept, near, cross):
    del before

    @pl.when(meets_far())
    def _():
        t = lax.axis_index("tgt")
        sent[...] = contract_turned(piece[...], grads[part_of(1 - t, half), :])
        kept[...] = contract_turned(piece[...], grads[part_of(t, half), :])
        for to, index in ((near, t), (cross, 1 - t)):
            to[:, part_of(t, half)] = kept[part_of(index, width), :]
            to[:, part_of(1 - t, half)] = sent[part_of(index, width), :]


def hand_on_kernel(half, scale, third, got, sent, near, cross, tile, back, *outs):
    finish_kernel([back.shape[0]], half, scale, None, third, got, tile, back)
    for value, out in zip((sent, near, cross), outs):
        out[...] = value[...]


def finish_kernel(widths, half, scale, before, *refs):
    del before
    *ins, tile, back = refs
    t = lax.axis_index("tgt")
    at, total = 0, sum(widths)
    for i, width in enumerate(widths):
        kept, got = ins[2 * i : 2 * i + 2]
        value = ((kept[...] + got[...]) * scale).astype(jnp.bfloat16)
        for h in range(2):
            tile[h * total + at : h * total + at + width, :] = value[h * width : (h + 1) * width]
        back[at : at + width, part_of(1 - t, half)] = value[2 * width :]
        at += width
    back[:, part_of(t, half)] = tile[part_of(t, total), :]


def early_finish_kernel(widths, half, scale, flat, before, *refs):
    *ins, tile, back = refs
    total = sum(widths)
    finish_kernel(widths, half, scale, before, *ins, tile, back.at[pl.ds(0, total)])
    back[total:, :] = flat[...]


def meets_far():
    place = lax.rem(lax.axis_index("blk"), 4)
    return (place == 0) | (place == 3)


def own_slot():
    return jnp.where(meets_far(), 2, 1)


def most_kernel(
    half, edge, self_tile, tile, flat, flat_before, back, tiles, partial, turned, far, sems
):
    slot = own_slot()
    whole = pltpu.make_async_copy(self_tile, tiles.at[0], sems.at[0])
    whole.start()
    copies, size = [], tile.shape[0] // 2
    returned = pltpu.make_async_copy(
        back.at[pl.ds(0, size)], tiles.at[3 - slot, pl.ds(0, size)], sems.at[3]
    )
    returned.start()
    far[:size, :] = back[:size, :]
    far[size:, :] = jnp.zeros((half - size, far.shape[1]), far.dtype)
    value = contract(flat[...], self_tile[...]) + contract(back[size:, :], far[...])
    for h in range(2):
        part = tile[h * size : h * size + edge, :]
        turned[h] = part.T
        copies.append(
            pltpu.make_async_copy(
                turned.at[h], tiles.at[slot, :, pl.ds(h * half, edge)], sems.at[1 + h]
            )
        )
        copies[h].start()
        value += multiply(flat_before[:, h * half : h * half + edge], part)
    partial[...] = value
    whole.wait()
    returned.wait()
    for copy in copies:
        copy.wait()


def last_kernel(
    half, edge, scale, before, got, cross, near, kept, partial, early, third, back_early,
    back_third, flat_before, near_new, near_back, tiles, influence, turned, far, late, total, sems,
):
    del before
    slot = own_slot()
    width = near.shape[0]
    first, second = early.shape[0] // 2, third.shape[0] // 2
    done = first + second
    copies = []

    def copy(source, target):
        copies.append(pltpu.make_async_copy(source, target, sems.at[len(copies)]))
        copies[-1].start()

    far[: first - edge, :] = jnp.zeros((first - edge, far.shape[1]), far.dtype)
    far[first - edge : done - edge, :] = back_third[...]
    summed = ((near[...] + cross[...]) * scale).astype(jnp.bfloat16)
    far[done - edge :, :] = jnp.where(meets_far(), near_back[...], summed)
    copy(
        far.at[pl.ds(first - edge, second + width)], tiles.at[3 - slot, pl.ds(first, second + width)]
    )
    new = ((kept[...] + got[...]) * scale).astype(jnp.bfloat16)
    new = jnp.where(meets_far(), new, near_new[...])
    value = partial[...]
    for h in range(2):
        start = h * half
        late[h, : first - edge, :] = early[h * first + edge : (h + 1) * first, :]
        late[h, first - edge : done - edge, :] = third[h * second : (h + 1) * second, :]
        late[h, done - edge :, :] = new[h * width : (h + 1) * width]
        turned[h] = late[h].T
        copy(turned.at[h], tiles.at[slot, :, pl.ds(start + edge, half - edge)])
        value += multiply(flat_before[:, start + edge : start + half], late[h])
    total[:, :edge] = value[:, :edge]
    total[:, edge:] = value[:, edge:] + contract(back_early[first:, :], far[...])
    copy(total, influence)
    for each in copies:
        each.wait()


def per_device(gradients, targets):
    blocks, groups = lax.axis_size("blk"), lax.axis_size("tgt")
    rows, features = gradients.shape
    columns = targets.shape[1]
    half = rows // groups
    scale = 1.0 / (features * groups) ** 0.5
    forward = [(b, b - b % 4 + AFTER[b % 4]) for b in range(blocks)]
    back = [(b, b - b % 4 + BEFORE[b % 4]) for b in range(blocks)]
    across = [(t, 1 - t) for t in range(groups)]
    beside = [(b, b ^ 1) for b in range(blocks)]
    back_across = [
        (b * groups + t, c * groups + (1 - t if b % 4 in (0, 3) else t))
        for b, c in back
        for t in range(groups)
    ]

    def f32(*shape):
        return jax.ShapeDtypeStruct(shape, jnp.float32)

    def b16(*shape):
        return jax.ShapeDtypeStruct(shape, jnp.bfloat16)

    widths = [half * n // 16 for n in SIXTEENTHS]
    spans = [(sum(widths[:i]), w) for i, w in enumerate(widths)]
    first = spans[-2][0]
    edge = half // 2
    flat = targets.T

    piece, mark = call(
        functools.partial(first_kernel, widths[0], half),
        [b16(2 * widths[0], features), f32(8, 128)],
        [ANY],
        [ANY, VMEM],
        [pltpu.SemaphoreType.DMA((2,))],
        vmem=FIRST_VMEM,
    )(gradients)
    gradients = call(
        load_kernel,
        b16(rows, features),
        [ANY] * 2,
        ANY,
        [pltpu.SemaphoreType.DMA((4,))],
        vmem=48,
    )(gradients, mark)
    sent, kept = call(
        functools.partial(self_kernel, half), [f32(half, rows)] * 2, [VMEM, ANY], [VMEM] * 2
    )(gradients, mark)
    pieces = call(
        functools.partial(rest_kernel, spans[1:], half),
        [b16(2 * w, features) for w in widths[1:]],
        [ANY] * 2,
        [ANY] * len(widths[1:]),
        [pltpu.SemaphoreType.DMA((2 * len(widths[1:]),))],
    )(gradients, kept)
    got = [lax.ppermute(piece, "blk", forward) for piece in (piece, *pieces)]
    self_tile = call(
        functools.partial(self_finish_kernel, scale), b16(half, rows), [VMEM] * 2, VMEM
    )(kept, lax.ppermute(sent, "tgt", across))

    def pair(width, piece, after):
        sent, kept = call(
            functools.partial(pair_kernel, width, half),
            [f32(3 * width, half)] * 2,
            [VMEM] * 2 + [ANY],
            [VMEM] * 2,
        )(piece, gradients, after)
        return [kept, lax.ppermute(sent, "tgt", across)]

    flat_before = lax.ppermute(flat, "blk", forward)
    near_sums = pair(widths[-1], lax.ppermute(pieces[-1], "blk", beside), mark)
    near_new, near_back = call(
        functools.partial(finish_kernel, widths[-1:], half, scale),
        [b16(2 * widths[-1], half), b16(widths[-1], rows)],
        [ANY] + [VMEM] * 2,
        [VMEM] * 2,
    )(mark, *near_sums)
    near_back = lax.ppermute(near_back, "blk", beside)
    sums = pair(widths[0], got[0], near_back)
    for w, piece in zip(widths[1:-2], got[1:-2]):
        sums += pair(w, piece, mark)
    sums += pair(widths[-2], got[-2], self_tile)

    some = widths[:EARLY]
    early, back_early = call(
        functools.partial(early_finish_kernel, some, half, scale),
        [b16(2 * sum(some), half), b16(sum(some) + columns, rows)],
        [VMEM, ANY] + [VMEM] * (2 * EARLY),
        [VMEM] * 2,
    )(flat, sums[-2], *sums[: 2 * EARLY])
    back_early = lax.ppermute(back_early, "blk", back)
    *_, second, width = widths
    shapes = [f32(2 * width, half)] + [f32(width, rows)] * 2
    sent, kept, near, cross = call(
        functools.partial(last_pair_kernel, width, half),
        [shapes[0], *shapes],
        [VMEM] * 2 + [ANY],
        [VMEM] * 4,
    )(got[-1], gradients, early)
    third, back_third, sent, near, cross = call(
        functools.partial(hand_on_kernel, half, scale),
        [b16(2 * second, half), b16(second, rows), *shapes],
        [VMEM] * 5,
        [VMEM] * 5,
        flops=FLOPS,
    )(*sums[2 * EARLY :], sent, near, cross)
    sent = lax.ppermute(sent, "tgt", across)
    near = lax.ppermute(near, "blk", back)
    cross = lax.ppermute(cross, ("blk", "tgt"), back_across)
    back_third = lax.ppermute(back_third, "blk", back)

    tiles, partial = call(
        functools.partial(most_kernel, half, edge),
        [b16(3, half, rows), f32(columns, half)],
        [VMEM] * 5,
        [ANY, VMEM],
        [
            pltpu.VMEM((2, half, edge), jnp.bfloat16),
            pltpu.VMEM((half, rows), jnp.bfloat16),
            pltpu.SemaphoreType.DMA((4,)),
        ],
    )(self_tile, early, flat, flat_before, back_early)
    tiles, influence = call(
        functools.partial(last_kernel, half, edge, scale),
        [b16(3, half, rows), f32(columns, half)],
        [ANY] + [VMEM] * 12,
        [ANY] * 2,
        [
            pltpu.VMEM((2, half, half - edge), jnp.bfloat16),
            pltpu.VMEM((half - edge, rows), jnp.bfloat16),
            pltpu.VMEM((2, half - edge, half), jnp.bfloat16),
            pltpu.VMEM((columns, half), jnp.float32),
            pltpu.SemaphoreType.DMA((5,)),
        ],
        {0: 0},
    )(
        tiles, sent, cross, near, kept, partial, early, third, back_early, back_third,
        flat_before, near_new, near_back,
    )
    return tiles, influence.T


def solution(mesh):
    return jax.shard_map(
        per_device,
        mesh=mesh,
        in_specs=(P("blk", "tgt"), P("blk", None)),
        out_specs=(P(None, ("blk", "tgt"), None), P(("blk", "tgt"), None)),
        check_vma=False,
    )
```

```python
import functools

import jax
import jax.numpy as jnp
from jax import lax
from jax.experimental import pallas as pl
from jax.experimental.pallas import tpu as pltpu
from jax.sharding import PartitionSpec as P

AFTER = {0: 1, 1: 3, 3: 2, 2: 0}
BEFORE = {after: before for before, after in AFTER.items()}
SIXTEENTHS = (6, 4, 2, 2, 2)
EARLY = 3
FIRST_VMEM = 50
FLOPS = 3000000000
VMEM = pl.BlockSpec(memory_space=pltpu.VMEM)
ANY = pl.BlockSpec(memory_space=pl.ANY)


def call(kernel, out, in_specs, out_specs, scratch=(), aliases=None, vmem=16, flops=0):
    return pl.pallas_call(
        kernel,
        out_shape=out,
        in_specs=in_specs,
        out_specs=out_specs,
        scratch_shapes=scratch,
        input_output_aliases=aliases or {},
        cost_estimate=pl.CostEstimate(flops=flops, bytes_accessed=0, transcendentals=0),
        compiler_params=pltpu.CompilerParams(vmem_limit_bytes=vmem * 2**20),
    )


def contract(left, right):
    return lax.dot_general(
        left, right, (((1,), (1,)), ((), ())), preferred_element_type=jnp.float32
    )


def multiply(left, right):
    return jnp.dot(left, right, preferred_element_type=jnp.float32)


def contract_turned(left, right):
    return contract(right, left).T


def part_of(index, size):
    return pl.ds(pl.multiple_of(index * size, size), size)


def run_copies(copies, sems):
    copies = [pltpu.make_async_copy(*ends, sems.at[i]) for i, ends in enumerate(copies)]
    for copy in copies:
        copy.start()
    for copy in copies:
        copy.wait()


def first_kernel(width, half, grads, out, mark, sems):
    run_copies(
        [
            (grads.at[pl.ds(h * half, width)], out.at[pl.ds(h * width, width)])
            for h in range(2)
        ],
        sems,
    )
    mark[...] = jnp.zeros_like(mark)


def load_kernel(grads, before, out, sems):
    del before
    size = grads.shape[0] // 4
    parts = [pl.ds(i * size, size) for i in range(4)]
    run_copies([(grads.at[part], out.at[part]) for part in parts], sems)


def rest_kernel(spans, half, grads, before, *refs):
    del before
    *outs, sems = refs
    run_copies(
        [
            (grads.at[pl.ds(h * half + at, width)], out.at[pl.ds(h * width, width)])
            for (at, width), out in zip(spans, outs)
            for h in range(2)
        ],
        sems,
    )


def self_kernel(half, grads, before, sent, kept):
    del before
    t = lax.axis_index("tgt")
    sent[...] = contract(grads[part_of(1 - t, half), :], grads[...])
    kept[...] = contract(grads[part_of(t, half), :], grads[...])


def self_finish_kernel(scale, kept, got, tile):
    tile[...] = ((kept[...] + got[...]) * scale).astype(jnp.bfloat16)


def share(sent, kept, width):
    t = lax.axis_index("tgt")
    sent[2 * width :, :] = kept[part_of(1 - t, width), :]
    kept[2 * width :, :] = sent[part_of(t, width), :]


def pair_kernel(width, half, piece, grads, before, sent, kept):
    del before
    t = lax.axis_index("tgt")
    product = contract_turned if 2 * width <= 128 else contract
    sent[: 2 * width, :] = product(piece[...], grads[part_of(1 - t, half), :])
    kept[: 2 * width, :] = product(piece[...], grads[part_of(t, half), :])
    share(sent, kept, width)


def last_pair_kernel(width, half, piece, grads, before, sent, kept, near, cross):
    del before

    @pl.when(meets_far())
    def _():
        t = lax.axis_index("tgt")
        sent[...] = contract_turned(piece[...], grads[part_of(1 - t, half), :])
        kept[...] = contract_turned(piece[...], grads[part_of(t, half), :])
        for to, index in ((near, t), (cross, 1 - t)):
            to[:, part_of(t, half)] = kept[part_of(index, width), :]
            to[:, part_of(1 - t, half)] = sent[part_of(index, width), :]


def hand_on_kernel(half, scale, third, got, sent, near, cross, tile, back, *outs):
    finish_kernel([back.shape[0]], half, scale, None, third, got, tile, back)
    for value, out in zip((sent, near, cross), outs):
        out[...] = value[...]


def finish_kernel(widths, half, scale, before, *refs):
    del before
    *ins, tile, back = refs
    t = lax.axis_index("tgt")
    at, total = 0, sum(widths)
    for i, width in enumerate(widths):
        kept, got = ins[2 * i : 2 * i + 2]
        value = ((kept[...] + got[...]) * scale).astype(jnp.bfloat16)
        for h in range(2):
            tile[h * total + at : h * total + at + width, :] = value[h * width : (h + 1) * width]
        back[at : at + width, part_of(1 - t, half)] = value[2 * width :]
        at += width
    back[:, part_of(t, half)] = tile[part_of(t, total), :]


def early_finish_kernel(widths, half, scale, flat, before, *refs):
    *ins, tile, back = refs
    total = sum(widths)
    finish_kernel(widths, half, scale, before, *ins, tile, back.at[pl.ds(0, total)])
    back[total:, :] = flat[...]


def meets_far():
    place = lax.rem(lax.axis_index("blk"), 4)
    return (place == 0) | (place == 3)


def own_slot():
    return jnp.where(meets_far(), 2, 1)


def most_kernel(
    half, edge, self_tile, tile, flat, flat_before, back, tiles, partial, turned, far, sems
):
    slot = own_slot()
    whole = pltpu.make_async_copy(self_tile, tiles.at[0], sems.at[0])
    whole.start()
    copies, size = [], tile.shape[0] // 2
    returned = pltpu.make_async_copy(
        back.at[pl.ds(0, size)], tiles.at[3 - slot, pl.ds(0, size)], sems.at[3]
    )
    returned.start()
    far[:size, :] = back[:size, :]
    far[size:, :] = jnp.zeros((half - size, far.shape[1]), far.dtype)
    value = contract(flat[...], self_tile[...]) + contract(back[size:, :], far[...])
    for h in range(2):
        part = tile[h * size : h * size + edge, :]
        turned[h] = part.T
        copies.append(
            pltpu.make_async_copy(
                turned.at[h], tiles.at[slot, :, pl.ds(h * half, edge)], sems.at[1 + h]
            )
        )
        copies[h].start()
        value += multiply(flat_before[:, h * half : h * half + edge], part)
    partial[...] = value
    whole.wait()
    returned.wait()
    for copy in copies:
        copy.wait()


def last_kernel(
    half, edge, scale, before, got, cross, near, kept, partial, early, third, back_early,
    back_third, flat_before, near_new, near_back, tiles, influence, turned, far, late, total, sems,
):
    del before
    slot = own_slot()
    width = near.shape[0]
    first, second = early.shape[0] // 2, third.shape[0] // 2
    done = first + second
    copies = []

    def copy(source, target):
        copies.append(pltpu.make_async_copy(source, target, sems.at[len(copies)]))
        copies[-1].start()

    far[: first - edge, :] = jnp.zeros((first - edge, far.shape[1]), far.dtype)
    far[first - edge : done - edge, :] = back_third[...]
    summed = ((near[...] + cross[...]) * scale).astype(jnp.bfloat16)
    far[done - edge :, :] = jnp.where(meets_far(), near_back[...], summed)
    copy(
        far.at[pl.ds(first - edge, second + width)], tiles.at[3 - slot, pl.ds(first, second + width)]
    )
    new = ((kept[...] + got[...]) * scale).astype(jnp.bfloat16)
    new = jnp.where(meets_far(), new, near_new[...])
    value = partial[...]
    for h in range(2):
        start = h * half
        late[h, : first - edge, :] = early[h * first + edge : (h + 1) * first, :]
        late[h, first - edge : done - edge, :] = third[h * second : (h + 1) * second, :]
        late[h, done - edge :, :] = new[h * width : (h + 1) * width]
        turned[h] = late[h].T
        copy(turned.at[h], tiles.at[slot, :, pl.ds(start + edge, half - edge)])
        value += multiply(flat_before[:, start + edge : start + half], late[h])
    total[:, :edge] = value[:, :edge]
    total[:, edge:] = value[:, edge:] + contract(back_early[first:, :], far[...])
    copy(total, influence)
    for each in copies:
        each.wait()


def per_device(gradients, targets):
    blocks, groups = lax.axis_size("blk"), lax.axis_size("tgt")
    rows, features = gradients.shape
    columns = targets.shape[1]
    half = rows // groups
    scale = 1.0 / (features * groups) ** 0.5
    forward = [(b, b - b % 4 + AFTER[b % 4]) for b in range(blocks)]
    back = [(b, b - b % 4 + BEFORE[b % 4]) for b in range(blocks)]
    across = [(t, 1 - t) for t in range(groups)]
    beside = [(b, b ^ 1) for b in range(blocks)]
    back_across = [
        (b * groups + t, c * groups + (1 - t if b % 4 in (0, 3) else t))
        for b, c in back
        for t in range(groups)
    ]

    def f32(*shape):
        return jax.ShapeDtypeStruct(shape, jnp.float32)

    def b16(*shape):
        return jax.ShapeDtypeStruct(shape, jnp.bfloat16)

    widths = [half * n // 16 for n in SIXTEENTHS]
    spans = [(sum(widths[:i]), w) for i, w in enumerate(widths)]
    first = spans[-2][0]
    edge = half // 2
    flat = targets.T

    piece, mark = call(
        functools.partial(first_kernel, widths[0], half),
        [b16(2 * widths[0], features), f32(8, 128)],
        [ANY],
        [ANY, VMEM],
        [pltpu.SemaphoreType.DMA((2,))],
        vmem=FIRST_VMEM,
    )(gradients)
    gradients = call(
        load_kernel,
        b16(rows, features),
        [ANY] * 2,
        ANY,
        [pltpu.SemaphoreType.DMA((4,))],
        vmem=48,
    )(gradients, mark)
    sent, kept = call(
        functools.partial(self_kernel, half), [f32(half, rows)] * 2, [VMEM, ANY], [VMEM] * 2
    )(gradients, mark)
    pieces = call(
        functools.partial(rest_kernel, spans[1:], half),
        [b16(2 * w, features) for w in widths[1:]],
        [ANY] * 2,
        [ANY] * len(widths[1:]),
        [pltpu.SemaphoreType.DMA((2 * len(widths[1:]),))],
    )(gradients, kept)
    got = [lax.ppermute(piece, "blk", forward) for piece in (piece, *pieces)]
    self_tile = call(
        functools.partial(self_finish_kernel, scale), b16(half, rows), [VMEM] * 2, VMEM
    )(kept, lax.ppermute(sent, "tgt", across))

    def pair(width, piece, after):
        sent, kept = call(
            functools.partial(pair_kernel, width, half),
            [f32(3 * width, half)] * 2,
            [VMEM] * 2 + [ANY],
            [VMEM] * 2,
        )(piece, gradients, after)
        return [kept, lax.ppermute(sent, "tgt", across)]

    flat_before = lax.ppermute(flat, "blk", forward)
    near_sums = pair(widths[-1], lax.ppermute(pieces[-1], "blk", beside), mark)
    near_new, near_back = call(
        functools.partial(finish_kernel, widths[-1:], half, scale),
        [b16(2 * widths[-1], half), b16(widths[-1], rows)],
        [ANY] + [VMEM] * 2,
        [VMEM] * 2,
    )(mark, *near_sums)
    near_back = lax.ppermute(near_back, "blk", beside)
    sums = pair(widths[0], got[0], near_back)
    for w, piece in zip(widths[1:-2], got[1:-2]):
        sums += pair(w, piece, mark)
    sums += pair(widths[-2], got[-2], self_tile)

    some = widths[:EARLY]
    early, back_early = call(
        functools.partial(early_finish_kernel, some, half, scale),
        [b16(2 * sum(some), half), b16(sum(some) + columns, rows)],
        [VMEM, ANY] + [VMEM] * (2 * EARLY),
        [VMEM] * 2,
    )(flat, sums[-2], *sums[: 2 * EARLY])
    back_early = lax.ppermute(back_early, "blk", back)
    *_, second, width = widths
    shapes = [f32(2 * width, half)] + [f32(width, rows)] * 2
    sent, kept, near, cross = call(
        functools.partial(last_pair_kernel, width, half),
        [shapes[0], *shapes],
        [VMEM] * 2 + [ANY],
        [VMEM] * 4,
    )(got[-1], gradients, early)
    third, back_third, sent, near, cross = call(
        functools.partial(hand_on_kernel, half, scale),
        [b16(2 * second, half), b16(second, rows), *shapes],
        [VMEM] * 5,
        [VMEM] * 5,
        flops=FLOPS,
    )(*sums[2 * EARLY :], sent, near, cross)
    sent = lax.ppermute(sent, "tgt", across)
    near = lax.ppermute(near, "blk", back)
    cross = lax.ppermute(cross, ("blk", "tgt"), back_across)
    back_third = lax.ppermute(back_third, "blk", back)

    tiles, partial = call(
        functools.partial(most_kernel, half, edge),
        [b16(3, half, rows), f32(columns, half)],
        [VMEM] * 5,
        [ANY, VMEM],
        [
            pltpu.VMEM((2, half, edge), jnp.bfloat16),
            pltpu.VMEM((half, rows), jnp.bfloat16),
            pltpu.SemaphoreType.DMA((4,)),
        ],
    )(self_tile, early, flat, flat_before, back_early)
    tiles, influence = call(
        functools.partial(last_kernel, half, edge, scale),
        [b16(3, half, rows), f32(columns, half)],
        [ANY] + [VMEM] * 12,
        [ANY] * 2,
        [
            pltpu.VMEM((2, half, half - edge), jnp.bfloat16),
            pltpu.VMEM((half - edge, rows), jnp.bfloat16),
            pltpu.VMEM((2, half - edge, half), jnp.bfloat16),
            pltpu.VMEM((columns, half), jnp.float32),
            pltpu.SemaphoreType.DMA((5,)),
        ],
        {0: 0},
    )(
        tiles, sent, cross, near, kept, partial, early, third, back_early, back_third,
        flat_before, near_new, near_back,
    )
    return tiles, influence.T


def solution(mesh):
    return jax.shard_map(
        per_device,
        mesh=mesh,
        in_specs=(P("blk", "tgt"), P("blk", None)),
        out_specs=(P(None, ("blk", "tgt"), None), P(("blk", "tgt"), None)),
        check_vma=False,
    )
```
